256 devices in a mesh: space: 32 (over x, y, z_lo), chan: 8 (over z_hi, core).
Axes of the slice: x: 4, y: 4, z: 8 (z_hi: 4, z_lo: 2; z = z_hi * 2 + z_lo), core: 2. Of those that a mesh axis runs over, the one named last changes fastest.
Arguments:
- volume: bfloat16 [128, 128, 1024], P('chan', 'space'), may hold values from -6 to 6
- conv_in: bfloat16 [27, 256, 128], P(None, 'chan'), may hold values from -0.109375 to 0.109375
- conv_group: bfloat16 [27, 256, 8], P(None, 'chan'), may hold values from -0.4375 to 0.4375
- cotangent: bfloat16 [256, 64, 256], P('chan', 'space'), may hold values from -6 to 6
Outputs:
- mixed_out: bfloat16 [256, 64, 256], P('chan', 'space')
- input_grad: float32 [128, 128, 1024], P('chan', 'space')
- filter_grad: float32 [27, 256, 128], P(None, 'chan')
- group_grad: float32 [27, 256, 8], P(None, 'chan')
The draws below stay inside these ranges and needn't reach their ends.
All inputs are finite; a program needn't handle non-finite values.
Results may differ from the reference program's by a relative error of at most 0.005.
Values may be sent and summed in bfloat16 or wider, within the bound.
No kernel may reach another device: no remote copies, remote signals or barrier semaphores. Data moves between devices by JAX's collectives and lax.ppermute only.
A program may use at most 64 MiB of HBM per device.

```python
import math
import jax
import jax.numpy as jnp
from jax import lax

C0 = 128
C1 = 256
GROUPS = 32
SIDE = 16
GW = 8
NZ = 64


def level_of(key, shape, pieces, smallest, top_value):
    factor_of = 1.0
    for axis_at, blocks in pieces:
        steps = jax.random.uniform(jax.random.fold_in(jax.random.fold_in(key, 6), axis_at), (blocks,), jnp.float32, smallest / len(pieces), top_value / len(pieces))
        factor_of = factor_of * jnp.repeat(jnp.exp(steps), shape[axis_at] // blocks).reshape((-1,) + (1,) * (len(shape) - 1 - axis_at))
    return factor_of


def centred(key, shape, width, limit, shards=(), kind=jnp.bfloat16):
    loudness = level_of(key, shape, shards, -0.22, 0.18) if shards else 1.0
    result = jax.random.normal(key, shape, jnp.float32) * width * loudness
    return jnp.minimum(jnp.maximum(result, -limit), limit).astype(kind)


def setup_inputs(seed: int = 0) -> dict:
    streams_of = jax.random.split(jax.random.key(seed), 5)
    return {
        "volume": centred(streams_of[0], (C0, 2 * NZ, 4 * SIDE * SIDE), 1.0, 6.0, ((0, 8), (1, 32))),
        "conv_in": centred(streams_of[1], (27, C1, C0), (27 * C0) ** -0.5, 0.109375, ((1, 8),)),
        "conv_group": centred(streams_of[2], (27, C1, GW), (27 * GW) ** -0.5, 0.4375, ((1, 8),)),
        "cotangent": centred(streams_of[3], (C1, NZ, SIDE * SIDE), 1.0, 6.0, ((0, 8), (1, 32))),
    }


OFFSETS = [(first, second, third) for first in (-1, 0, 1) for second in (-1, 0, 1) for third in (-1, 0, 1)]
PHASES = [(first, second, third) for first in (0, 1) for second in (0, 1) for third in (0, 1)]

def pick_phase(values, dim_index, offset):
    length = values.shape[dim_index]
    layout = values.shape[:dim_index] + (length // 2, 2) + values.shape[dim_index + 1:]
    picked = lax.index_in_dim(values.reshape(layout), 0 if offset == 0 else 1, dim_index + 1, keepdims=False)
    if offset < 0:
        picked = jnp.roll(picked, 1, dim_index)
    return picked

def stride_view(source, depth_k, row_k, col_k):
    picked = pick_phase(source, 1, depth_k)
    picked = pick_phase(picked, 2, row_k)
    return pick_phase(picked, 3, col_k)

def silu_grad(hidden):
    sigmoid_val = jax.nn.sigmoid(hidden)
    return sigmoid_val * (1.0 + hidden * (1.0 - sigmoid_val))

def reference(volume, conv_in, conv_group, cotangent):
    ordered = volume.reshape(C0, 2 * NZ, 2, 2, SIDE, SIDE).transpose(0, 1, 4, 2, 5, 3)
    inputs = ordered.reshape(C0, 2 * NZ, 2 * SIDE, 2 * SIDE)
    cell_count = NZ * SIDE * SIDE
    inverse_root = 1.0 / math.sqrt(cell_count)
    hidden = jnp.zeros((C1, cell_count), jnp.float32)
    for tap_index, offsets in enumerate(OFFSETS):
        window = stride_view(inputs, *offsets).reshape(C0, cell_count)
        hidden = hidden + jnp.dot(conv_in[tap_index], window, preferred_element_type=jnp.float32)
    active = (hidden * jax.nn.sigmoid(hidden)).astype(jnp.bfloat16)
    grouped = active.reshape(GROUPS, GW, NZ, SIDE, SIDE)
    upstream = cotangent.reshape(GROUPS, GW, NZ, SIDE, SIDE)
    flat_up = upstream.reshape(GROUPS, GW, cell_count).astype(jnp.float32)
    mixed = jnp.zeros((GROUPS, GW, cell_count), jnp.float32)
    act_grad = jnp.zeros((GROUPS, GW, cell_count), jnp.float32)
    group_terms = []
    for tap_index, (depth_k, row_k, col_k) in enumerate(OFFSETS):
        weights = conv_group[tap_index].reshape(GROUPS, GW, GW).astype(jnp.float32)
        shifted = jnp.roll(grouped, (-depth_k, -row_k, -col_k), (2, 3, 4)).reshape(GROUPS, GW, cell_count).astype(jnp.float32)
        backward_view = jnp.roll(upstream, (depth_k, row_k, col_k), (2, 3, 4)).reshape(GROUPS, GW, cell_count).astype(jnp.float32)
        mixed = mixed + jnp.einsum('goi,gic->goc', weights, shifted)
        act_grad = act_grad + jnp.einsum('goi,goc->gic', weights, backward_view)
        group_terms.append(jnp.einsum('goc,gic->goi', flat_up, shifted).reshape(C1, GW))
    mixed_out = mixed.reshape(C1, NZ, SIDE * SIDE).astype(jnp.bfloat16)
    group_grad = jnp.stack(group_terms) * inverse_root
    hidden_grad = (act_grad.reshape(C1, cell_count) * silu_grad(hidden)).astype(jnp.bfloat16)
    filter_terms = []
    phase_sums = {}
    for tap_index, (depth_k, row_k, col_k) in enumerate(OFFSETS):
        window = stride_view(inputs, depth_k, row_k, col_k).reshape(C0, cell_count)
        filter_terms.append(jnp.dot(hidden_grad, window.T, preferred_element_type=jnp.float32))
        contrib = jnp.dot(conv_in[tap_index].T, hidden_grad, preferred_element_type=jnp.float32).reshape(C0, NZ, SIDE, SIDE)
        for dim_index, offset in ((1, depth_k), (2, row_k), (3, col_k)):
            if offset < 0:
                contrib = jnp.roll(contrib, -1, dim_index)
        slot_key = (0 if depth_k == 0 else 1, 0 if row_k == 0 else 1, 0 if col_k == 0 else 1)
        phase_sums[slot_key] = phase_sums[slot_key] + contrib if slot_key in phase_sums else contrib
    stacked = jnp.stack([phase_sums[slot_key] for slot_key in PHASES]).reshape(2, 2, 2, C0, NZ, SIDE, SIDE)
    input_grad = stacked.transpose(3, 4, 0, 1, 2, 5, 6).reshape(C0, 2 * NZ, 4 * SIDE * SIDE)
    filter_grad = jnp.stack(filter_terms) * inverse_root
    return (mixed_out, input_grad, filter_grad, group_grad)
```

```python
import math

import jax
import jax.numpy as jnp
from jax import lax
from jax.experimental import pallas as pl
from jax.experimental.pallas import tpu as pltpu
from jax.sharding import PartitionSpec as P

OFFSETS = [
    (first, second, third) for first in (-1, 0, 1) for second in (-1, 0, 1) for third in (-1, 0, 1)
]
TAPS = len(OFFSETS)
BF16 = jnp.bfloat16
F32 = jnp.float32
VMEM_LIMIT = 48 * 1024 * 1024


def phase_of(row_k, col_k):
    return 2 * (row_k != 0) + (col_k != 0)


def roll_class(row_k, col_k):
    return 2 * (row_k < 0) + (col_k < 0)


def shift_cells(plane, row_k, col_k, side):
    square = side * side
    moved = plane
    if col_k:
        inside = pltpu.roll(moved, (-col_k) % square, 1)
        wrapped = pltpu.roll(moved, (col_k * (side - 1)) % square, 1)
        column = lax.broadcasted_iota(jnp.int32, moved.shape, 1) % side
        moved = jnp.where(column == (side - 1 if col_k > 0 else 0), wrapped, inside)
    if row_k:
        moved = pltpu.roll(moved, (-row_k * side) % square, 1)
    return moved


def call(kernel, outs, *args, scratch=(), flops=0, moved=0):
    whole = pl.BlockSpec(memory_space=pltpu.VMEM)
    single = not isinstance(outs, (tuple, list))
    return pl.pallas_call(
        kernel,
        out_shape=outs,
        in_specs=[
            pl.BlockSpec(memory_space=pltpu.SMEM) if arg.dtype == jnp.int32 else whole
            for arg in args
        ],
        out_specs=whole if single else [whole] * len(outs),
        scratch_shapes=list(scratch),
        compiler_params=pltpu.CompilerParams(vmem_limit_bytes=VMEM_LIMIT),
        cost_estimate=pl.CostEstimate(flops=flops, bytes_accessed=moved, transcendentals=0),
    )(*args)


def split_filter(conv_in, pieces):
    taps, outputs, inputs = conv_in.shape
    width = inputs // pieces

    def kernel(src, dst):
        for piece in range(pieces):
            dst[piece] = jnp.concatenate(
                [src[tap, :, piece * width : (piece + 1) * width] for tap in range(taps)], axis=1
            )

    return call(kernel, jax.ShapeDtypeStruct((pieces, outputs, taps * width), BF16), conv_in)


def fill_windows(planes, store, direction, side):
    count = len(planes) - 2
    for index, plane in enumerate(planes):
        plane = plane.astype(F32)
        for row_k in (-1, 0, 1):
            for col_k in (-1, 0, 1):
                window = shift_cells(plane, direction * row_k, direction * col_k, side).astype(BF16)
                for depth_k in (-1, 0, 1):
                    inner = index - 1 - direction * depth_k
                    if 0 <= inner < count:
                        tap = 9 * (depth_k + 1) + 3 * (row_k + 1) + col_k + 1
                        store(tap, inner, window)


def block_diagonal(values, width, outputs):
    rows = values.shape[0]
    tiled = jnp.concatenate([values] * (outputs // width), axis=1)
    row = lax.broadcasted_iota(jnp.int32, tiled.shape, 0) % outputs
    column = lax.broadcasted_iota(jnp.int32, tiled.shape, 1)
    return jnp.where(row // width == column // width, tiled, jnp.zeros_like(tiled))


def upstream_part(low, cotangent, high, conv_group, side):
    planes, outputs, square = cotangent.shape
    taps, _, width = conv_group.shape
    cells = planes * square

    def kernel(low_ref, mid_ref, high_ref, group_ref, grad_ref, windows_ref):
        def store(tap, inner, window):
            windows_ref[
                tap * outputs : (tap + 1) * outputs, inner * square : (inner + 1) * square
            ] = window

        fill_windows(
            [low_ref[...]] + [mid_ref[z] for z in range(planes)] + [high_ref[...]], store, -1, side
        )
        weights = block_diagonal(group_ref[...].astype(F32), width, outputs).astype(BF16)
        grad_ref[...] = lax.dot_general(
            weights, windows_ref[...], (((0,), (0,)), ((), ())), preferred_element_type=F32
        )

    return call(
        kernel,
        (
            jax.ShapeDtypeStruct((outputs, cells), F32),
            jax.ShapeDtypeStruct((taps * outputs, cells), BF16),
        ),
        low,
        cotangent,
        high,
        conv_group.reshape(taps * outputs, width),
    )


def mix_part(low, active, high, conv_group, side):
    outputs, cells = active.shape
    square = side * side
    planes = cells // square
    taps, _, width = conv_group.shape

    def kernel(low_ref, mid_ref, high_ref, group_ref, out_ref, windows_ref):
        def store(tap, inner, window):
            windows_ref[
                tap * outputs : (tap + 1) * outputs, inner * square : (inner + 1) * square
            ] = window

        middle = [mid_ref[:, z * square : (z + 1) * square] for z in range(planes)]
        fill_windows([low_ref[...]] + middle + [high_ref[...]], store, 1, side)
        weights = block_diagonal(group_ref[...].astype(F32), width, outputs).astype(BF16)
        weights = jnp.concatenate(
            [weights[tap * outputs : (tap + 1) * outputs] for tap in range(taps)], axis=1
        )
        mixed = jnp.dot(weights, windows_ref[...], preferred_element_type=F32).astype(BF16)
        for z in range(planes):
            out_ref[z] = mixed[:, z * square : (z + 1) * square]

    return call(
        kernel,
        jax.ShapeDtypeStruct((planes, outputs, square), BF16),
        low,
        active,
        high,
        conv_group.reshape(taps * outputs, width),
        scratch=[pltpu.VMEM((taps * outputs, cells), BF16)],
    )


def main_part(place, pieces, conv_in, act_grad, windows, width, rows, side):
    taps, outputs, inputs = conv_in.shape
    square = side * side
    cells = act_grad.shape[1]
    planes = cells // square
    frames = 2 * planes + 1
    depth = 12 * inputs
    filter_rows = taps * outputs
    group_rows = -(-filter_rows // 128) * width

    def kernel(*refs):
        place_ref, conv_ref, grad_ref, windows_ref = refs[:4]
        piece_refs = refs[4 : 4 + len(pieces)]
        active_ref, hidden_grad_ref, terms_ref, field, filters = refs[4 + len(pieces) :]
        for index, (ref, (_, parts)) in enumerate(zip(piece_refs, pieces)):
            base = pl.multiple_of(place_ref[index], 16)
            for source, frame, phase, lanes in parts:
                start = (frame * 4 + phase) * inputs
                field[pl.ds(start + base, 16), :] = ref[source, :, lanes : lanes + square]
        filters[...] = jnp.zeros_like(filters)
        places = []
        for tap, (depth_k, row_k, col_k) in enumerate(OFFSETS):
            top = roll_class(row_k, col_k) * outputs
            left = ((depth_k + 1) * 4 + phase_of(row_k, col_k)) * inputs
            places.append((slice(top, top + outputs), slice(left, left + inputs)))
            filters[places[-1]] = conv_ref[tap]
        terms = jnp.zeros((4 * outputs, depth), F32)
        actives = []
        for z in range(planes):
            view = field[8 * inputs * z : 8 * inputs * z + depth, :]
            sums = jnp.dot(filters[...], view, preferred_element_type=F32)
            hidden = sums[:outputs]
            for kind, (row_k, col_k) in ((1, (0, -1)), (2, (-1, 0)), (3, (-1, -1))):
                part = sums[kind * outputs : (kind + 1) * outputs]
                hidden = hidden + shift_cells(part, row_k, col_k, side)
            sigmoid = 1.0 / (1.0 + jnp.exp(-hidden))
            active = (hidden * sigmoid).astype(BF16)
            at = slice(z * square, (z + 1) * square)
            slope = sigmoid * (1.0 + hidden * (1.0 - sigmoid))
            grad = grad_ref[:, at] * slope
            active_ref[:, at] = active
            actives.append(active)
            rounded = grad.astype(BF16)
            hidden_grad_ref[:, at] = rounded
            grad = rounded.astype(F32)
            shifted = jnp.concatenate(
                [shift_cells(grad, row_k, col_k, side) for row_k in (0, 1) for col_k in (0, 1)],
                axis=0,
            ).astype(BF16)
            terms = terms + lax.dot_general(
                shifted, view, (((1,), (1,)), ((), ())), preferred_element_type=F32
            )
        for tap, at in enumerate(places):
            terms_ref[tap * outputs : (tap + 1) * outputs, :] = terms[at].astype(BF16)
        pairs = lax.dot_general(
            jnp.concatenate(actives, axis=1),
            windows_ref[...],
            (((1,), (1,)), ((), ())),
            preferred_element_type=F32,
        )
        group = lax.broadcasted_iota(jnp.int32, (width, filter_rows), 1) % outputs // width
        kept = jnp.zeros((width, filter_rows), F32)
        for index in range(outputs // width):
            block = pairs[index * width : (index + 1) * width]
            kept = kept + jnp.where(group == index, block, 0.0)
        short = group_rows // width * 128 - filter_rows
        kept = jnp.concatenate([kept, jnp.zeros((width, short), F32)], axis=1)
        tail = [kept[:, 128 * i : 128 * (i + 1)] for i in range(group_rows // width)]
        tail.append(jnp.zeros((rows - filter_rows - group_rows, 128), F32))
        terms_ref[filter_rows:, :] = jnp.concatenate(tail, axis=0).astype(BF16)

    arrays = [piece for piece, _ in pieces]
    return call(
        kernel,
        (
            jax.ShapeDtypeStruct((outputs, cells), BF16),
            jax.ShapeDtypeStruct((outputs, cells), BF16),
            jax.ShapeDtypeStruct((rows, 128), BF16),
        ),
        place,
        conv_in,
        act_grad,
        windows,
        *arrays,
        scratch=[
            pltpu.VMEM((frames * 4 * inputs, square), BF16),
            pltpu.VMEM((4 * outputs, depth), BF16),
        ],
    )


def input_part(columns, grad_all, width, side):
    square = side * side
    cells = grad_all.shape[1]
    planes = cells // square

    def kernel(columns_ref, grad_ref, out_ref, below_ref):
        terms = lax.dot_general(
            columns_ref[...], grad_ref[...], (((0,), (0,)), ((), ())), preferred_element_type=F32
        )
        sums = {}
        for tap, (depth_k, row_k, col_k) in enumerate(OFFSETS):
            for z in range(planes):
                key = (2 * z + depth_k, phase_of(row_k, col_k), roll_class(row_k, col_k))
                part = terms[tap * width : (tap + 1) * width, z * square : (z + 1) * square]
                sums[key] = sums[key] + part if key in sums else part
        total = {}
        for (frame, phase, kind), part in sums.items():
            part = shift_cells(part, kind // 2, kind % 2, side)
            key = (frame, phase)
            total[key] = total[key] + part if key in total else part
        for (frame, phase), part in total.items():
            at = slice(phase * square, (phase + 1) * square)
            if frame < 0:
                below_ref[:, at] = part.astype(BF16)
            else:
                out_ref[frame, :, at] = part

    return call(
        kernel,
        (
            jax.ShapeDtypeStruct((2 * planes, width, 4 * square), F32),
            jax.ShapeDtypeStruct((width, 4 * square), BF16),
        ),
        columns,
        grad_all,
    )


def sum_part(received, scale):
    devices, rows, lanes = received.shape

    def kernel(src, dst):
        total = src[0].astype(F32)
        for index in range(1, devices):
            total = total + src[index].astype(F32)
        total = total * scale
        for index in range(devices):
            dst[index] = total

    return call(kernel, jax.ShapeDtypeStruct(received.shape, F32), received)


def final_part(gathered, taps, outputs, width):
    rows = taps * outputs
    blocks = -(-rows // 128)

    def kernel(src, filter_ref, group_ref):
        filter_ref[...] = src[:rows, :].reshape(taps, outputs, 128)
        for index in range(blocks):
            block = src[rows + index * width : rows + (index + 1) * width, :]
            block = jnp.concatenate([block] * (128 // width), axis=0).T
            low = index * 128
            count = min(128, rows - low)
            group_ref[low : low + count, :] = block[:count, :width]

    return call(
        kernel,
        (
            jax.ShapeDtypeStruct((taps, outputs, 128), F32),
            jax.ShapeDtypeStruct((rows, width), F32),
        ),
        gathered,
    )


def body(volume, conv_in, conv_group, cotangent):
    in_chan, in_planes, flat_in = volume.shape
    side = math.isqrt(flat_in) // 2
    square = side * side
    planes = in_planes // 2
    cells = planes * square
    taps, outputs, inputs = conv_in.shape
    width = conv_group.shape[2]
    slabs = lax.axis_size("space")
    blocks = lax.axis_size("chan")

    def along_space(block, step):
        return lax.ppermute(block, "space", [(i, (i + step) % slabs) for i in range(slabs)])

    def along_chips(block, step):
        return lax.ppermute(
            block, "chan", [(i, (i + 2 * step) % blocks) for i in range(blocks)]
        )

    def other_core(block):
        return lax.ppermute(block, "chan", [(i, i ^ 1) for i in range(blocks)])

    framed = jnp.transpose(volume, (1, 0, 2))
    below = along_space(framed[in_planes - 1 :], 1)
    own = jnp.concatenate([below, framed], axis=0)
    from_low = along_chips(own, 1)
    from_high = along_chips(own, -1)
    half = flat_in // 2
    far_left = along_chips(from_low[:, :, :half], 1)
    far_right = along_chips(from_high[:, :, half:], -1)

    upstream = jnp.transpose(cotangent, (1, 0, 2))
    up_low = along_space(upstream[planes - 1], 1)
    up_high = along_space(upstream[0], -1)
    act_grad, windows = upstream_part(up_low, upstream, up_high, conv_group, side)

    columns = lax.all_to_all(
        split_filter(conv_in, blocks), "chan", split_axis=0, concat_axis=0, tiled=True
    ).reshape(blocks * outputs, taps * in_chan)

    frames = in_planes + 1
    all_parts = [(f, f, p, p * square) for f in range(frames) for p in range(4)]
    left_parts = [(f, f, p, p * square) for f in range(frames) for p in (0, 1)]
    right_parts = [(f, f, p, (p - 2) * square) for f in range(frames) for p in (2, 3)]
    same = [
        (own, all_parts, 0),
        (from_low, all_parts, -1),
        (from_high, all_parts, 1),
        (far_left, left_parts, 2),
        (far_right, right_parts, 2),
    ]
    me = lax.axis_index("chan")
    pieces, place = [], []
    for block, parts, step in same:
        owner = (me + 2 * step) % blocks
        pieces += [(block, parts), (other_core(block), parts)]
        place += [owner * in_chan, (owner ^ 1) * in_chan]
    place = jnp.stack(place).astype(jnp.int32)

    rows = -(-(taps * outputs + 64) // (slabs * 32)) * slabs * 32
    active, hidden_grad, terms = main_part(
        place, pieces, conv_in, act_grad, windows, width, rows, side
    )
    received = lax.all_to_all(
        terms.reshape(slabs, rows // slabs, 128), "space", split_axis=0, concat_axis=0, tiled=True
    )
    scale = 1.0 / math.sqrt(slabs * cells)
    gathered = lax.all_to_all(
        sum_part(received, scale), "space", split_axis=0, concat_axis=0, tiled=True
    )
    filter_grad, group_grad = final_part(gathered.reshape(rows, 128), taps, outputs, width)

    grad_all = lax.all_gather(hidden_grad, "chan", axis=0, tiled=True)
    framed_grad, grad_below = input_part(columns, grad_all, in_chan, side)
    returned = along_space(grad_below, -1).astype(F32)
    framed_grad = framed_grad.at[in_planes - 1].add(returned)
    input_grad = jnp.transpose(framed_grad, (1, 0, 2))

    act_low = along_space(active[:, cells - square :], 1)
    act_high = along_space(active[:, :square], -1)
    mixed = mix_part(act_low, active, act_high, conv_group, side)
    mixed_out = jnp.transpose(mixed, (1, 0, 2))
    return (mixed_out, input_grad, filter_grad, group_grad.reshape(taps, outputs, width))


def solution(mesh):
    return jax.shard_map(
        body,
        mesh=mesh,
        in_specs=(
            P("chan", "space", None),
            P(None, "chan", None),
            P(None, "chan", None),
            P("chan", "space", None),
        ),
        out_specs=(
            P("chan", "space", None),
            P("chan", "space", None),
            P(None, "chan", None),
            P(None, "chan", None),
        ),
        check_vma=False,
    )
```

```python
import math

import jax
import jax.numpy as jnp
from jax import lax
from jax.experimental import pallas as pl
from jax.experimental.pallas import tpu as pltpu
from jax.sharding import PartitionSpec as P

OFFSETS = [
    (first, second, third) for first in (-1, 0, 1) for second in (-1, 0, 1) for third in (-1, 0, 1)
]
TAPS = len(OFFSETS)
BF16 = jnp.bfloat16
F32 = jnp.float32
VMEM_LIMIT = 48 * 1024 * 1024


def phase_of(row_k, col_k):
    return 2 * (row_k != 0) + (col_k != 0)


def roll_class(row_k, col_k):
    return 2 * (row_k < 0) + (col_k < 0)


def shift_cells(plane, row_k, col_k, side):
    square = side * side
    moved = plane
    if col_k:
        inside = pltpu.roll(moved, (-col_k) % square, 1)
        wrapped = pltpu.roll(moved, (col_k * (side - 1)) % square, 1)
        column = lax.broadcasted_iota(jnp.int32, moved.shape, 1) % side
        moved = jnp.where(column == (side - 1 if col_k > 0 else 0), wrapped, inside)
    if row_k:
        moved = pltpu.roll(moved, (-row_k * side) % square, 1)
    return moved


def call(kernel, outs, *args, scratch=(), flops=0, moved=0):
    whole = pl.BlockSpec(memory_space=pltpu.VMEM)
    single = not isinstance(outs, (tuple, list))
    return pl.pallas_call(
        kernel,
        out_shape=outs,
        in_specs=[whole] * len(args),
        out_specs=whole if single else [whole] * len(outs),
        scratch_shapes=list(scratch),
        compiler_params=pltpu.CompilerParams(vmem_limit_bytes=VMEM_LIMIT),
        cost_estimate=pl.CostEstimate(flops=flops, bytes_accessed=moved, transcendentals=0),
    )(*args)


def prep_part(volume, cotangent):
    in_chan, in_planes, flat_in = volume.shape
    outputs, planes, square = cotangent.shape

    def kernel(vol_ref, cot_ref, own_ref, packed_ref, cells_ref):
        for frame in range(in_planes):
            for phase in range(4):
                low = (frame * 4 + phase) * in_chan
                part = vol_ref[frame, :, phase * square : (phase + 1) * square]
                own_ref[low : low + in_chan, :] = part
                if frame == in_planes - 1:
                    packed_ref[phase * in_chan : (phase + 1) * in_chan, :] = part
        for z in range(planes):
            cells_ref[z * outputs : (z + 1) * outputs, :] = cot_ref[z]
        packed_ref[4 * in_chan :, :] = cot_ref[planes - 1]

    return call(
        kernel,
        (
            jax.ShapeDtypeStruct((in_planes * 4 * in_chan, square), BF16),
            jax.ShapeDtypeStruct((4 * in_chan + outputs, square), BF16),
            jax.ShapeDtypeStruct((planes * outputs, square), BF16),
        ),
        jnp.transpose(volume, (1, 0, 2)),
        jnp.transpose(cotangent, (1, 0, 2)),
    )


def split_filter(conv_in, in_chan, square):
    taps, outputs, inputs = conv_in.shape
    count = inputs // in_chan
    block_rows = 2 * outputs
    short = 2 * square - taps * in_chan

    def kernel(conv_ref, here_ref, up_ref, down_ref, far_ref, blocks):
        me = lax.axis_index("chan")
        for owner in range(count):
            steps = lax.rem(owner // 2 + count // 2 - me // 2, count // 2)
            crossed = lax.rem(owner + me, 2)
            wide = [conv_ref[tap, :, owner * in_chan : (owner + 1) * in_chan] for tap in range(taps)]
            wide = jnp.concatenate(wide + [jnp.zeros((outputs, short), BF16)], axis=1)
            blocks[2 * steps + crossed, :outputs, :] = wide[:, :square]
            blocks[2 * steps + crossed, outputs:, :] = wide[:, square:]
        for ref, order in ((here_ref, (1, 0)), (up_ref, (2, 3)), (down_ref, (6, 7)), (far_ref, (4, 5))):
            for index, block in enumerate(order):
                ref[index * block_rows : (index + 1) * block_rows, :] = blocks[block]

    return call(
        kernel,
        [jax.ShapeDtypeStruct((2 * block_rows, square), BF16)] * 4,
        conv_in,
        scratch=[pltpu.VMEM((count, block_rows, square), BF16)],
    )


def fill_windows(planes, store, direction, side):
    count = len(planes) - 2
    for index, plane in enumerate(planes):
        plane = plane.astype(F32)
        for row_k in (-1, 0, 1):
            for col_k in (-1, 0, 1):
                window = shift_cells(plane, direction * row_k, direction * col_k, side).astype(BF16)
                for depth_k in (-1, 0, 1):
                    inner = index - 1 - direction * depth_k
                    if 0 <= inner < count:
                        tap = 9 * (depth_k + 1) + 3 * (row_k + 1) + col_k + 1
                        store(tap, inner, window)


def block_diagonal(values, outputs):
    width, columns = values.shape
    tiled = jnp.concatenate([values] * (outputs // width), axis=0)
    row = lax.broadcasted_iota(jnp.int32, tiled.shape, 0)
    column = lax.broadcasted_iota(jnp.int32, tiled.shape, 1) % outputs
    return jnp.where(row // width == column // width, tiled, jnp.zeros_like(tiled))


def upstream_part(packed, cotangent, high, group_filter, side):
    square = side * side
    taps, width, outputs = group_filter.shape
    planes = cotangent.shape[0] // outputs
    cells = planes * square
    skipped = packed.shape[0] - outputs

    def kernel(low_ref, mid_ref, high_ref, group_ref, grad_ref, windows_ref):
        def store(tap, inner, window):
            windows_ref[
                tap * outputs : (tap + 1) * outputs, inner * square : (inner + 1) * square
            ] = window

        middle = [mid_ref[z * outputs : (z + 1) * outputs, :] for z in range(planes)]
        fill_windows([low_ref[skipped:, :]] + middle + [high_ref[...]], store, -1, side)
        flat = jnp.concatenate([group_ref[tap].astype(F32) for tap in range(taps)], axis=1)
        weights = block_diagonal(flat, outputs).astype(BF16)
        grad_ref[...] = jnp.dot(weights, windows_ref[...], preferred_element_type=F32)

    return call(
        kernel,
        (
            jax.ShapeDtypeStruct((outputs, cells), F32),
            jax.ShapeDtypeStruct((taps * outputs, cells), BF16),
        ),
        packed,
        cotangent,
        high,
        group_filter,
    )


def owner_row(step, other, rows):
    me = lax.axis_index("chan")
    count = lax.axis_size("chan")
    owner = lax.rem(me + (2 * step) % count, count)
    if other:
        owner = owner + 1 - 2 * lax.rem(owner, 2)
    return pl.multiple_of(owner * rows, rows)


def main_part(pieces, conv_in, act_grad, windows, width, rows, side):
    taps, outputs, inputs = conv_in.shape
    square = side * side
    cells = act_grad.shape[1]
    planes = cells // square
    frames = 2 * planes + 1
    depth = 12 * inputs
    in_chan = inputs // lax.axis_size("chan")
    filter_rows = taps * outputs
    group_rows = -(-filter_rows // 128) * width

    def kernel(*refs):
        conv_ref, grad_ref, windows_ref = refs[:3]
        piece_refs = refs[3 : 3 + len(pieces)]
        active_ref, hidden_grad_ref, terms_ref, field, filters = refs[3 + len(pieces) :]
        for ref, (_, parts) in zip(piece_refs, pieces):
            for first, slots, step, other in parts:
                base = owner_row(step, other, in_chan)
                for index, slot in enumerate(slots):
                    low = first + index * in_chan
                    field[pl.ds(slot * inputs + base, in_chan), :] = ref[low : low + in_chan, :]
        filters[...] = jnp.zeros_like(filters)
        places = []
        for tap, (depth_k, row_k, col_k) in enumerate(OFFSETS):
            top = roll_class(row_k, col_k) * outputs
            left = ((depth_k + 1) * 4 + phase_of(row_k, col_k)) * inputs
            places.append((slice(top, top + outputs), slice(left, left + inputs)))
            filters[places[-1]] = conv_ref[tap]
        terms = jnp.zeros((4 * outputs, depth), F32)
        actives = []
        for z in range(planes):
            view = field[8 * inputs * z : 8 * inputs * z + depth, :]
            sums = jnp.dot(filters[...], view, preferred_element_type=F32)
            hidden = sums[:outputs]
            for kind, (row_k, col_k) in ((1, (0, -1)), (2, (-1, 0)), (3, (-1, -1))):
                part = sums[kind * outputs : (kind + 1) * outputs]
                hidden = hidden + shift_cells(part, row_k, col_k, side)
            sigmoid = 1.0 / (1.0 + jnp.exp(-hidden))
            active = (hidden * sigmoid).astype(BF16)
            at = slice(z * square, (z + 1) * square)
            slope = sigmoid * (1.0 + hidden * (1.0 - sigmoid))
            grad = grad_ref[:, at] * slope
            active_ref[:, at] = active
            actives.append(active)
            rounded = grad.astype(BF16)
            hidden_grad_ref[z * outputs : (z + 1) * outputs, :] = rounded
            grad = rounded.astype(F32)
            shifted = jnp.concatenate(
                [shift_cells(grad, row_k, col_k, side) for row_k in (0, 1) for col_k in (0, 1)],
                axis=0,
            ).astype(BF16)
            terms = terms + lax.dot_general(
                shifted, view, (((1,), (1,)), ((), ())), preferred_element_type=F32
            )
        for tap, at in enumerate(places):
            terms_ref[tap * outputs : (tap + 1) * outputs, :] = terms[at].astype(BF16)
        pairs = lax.dot_general(
            jnp.concatenate(actives, axis=1),
            windows_ref[...],
            (((1,), (1,)), ((), ())),
            preferred_element_type=F32,
        )
        group = lax.broadcasted_iota(jnp.int32, (width, filter_rows), 1) % outputs // width
        kept = jnp.zeros((width, filter_rows), F32)
        for index in range(outputs // width):
            block = pairs[index * width : (index + 1) * width]
            kept = kept + jnp.where(group == index, block, 0.0)
        short = group_rows // width * 128 - filter_rows
        kept = jnp.concatenate([kept, jnp.zeros((width, short), F32)], axis=1)
        tail = [kept[:, 128 * i : 128 * (i + 1)] for i in range(group_rows // width)]
        tail.append(jnp.zeros((rows - filter_rows - group_rows, 128), F32))
        terms_ref[filter_rows:, :] = jnp.concatenate(tail, axis=0).astype(BF16)

    return call(
        kernel,
        (
            jax.ShapeDtypeStruct((outputs, cells), BF16),
            jax.ShapeDtypeStruct((planes * outputs, square), BF16),
            jax.ShapeDtypeStruct((rows, 128), BF16),
        ),
        conv_in,
        act_grad,
        windows,
        *[piece for piece, _ in pieces],
        scratch=[
            pltpu.VMEM((frames * 4 * inputs, square), BF16),
            pltpu.VMEM((4 * outputs, depth), BF16),
        ],
    )


def input_part(pieces, active, width, side):
    square = side * side
    outputs, cells = active.shape
    planes = cells // square
    devices = lax.axis_size("chan")

    def kernel(active_ref, *refs):
        piece_refs = refs[: len(pieces)]
        out_ref, down_ref, grads, filters = refs[len(pieces) :]
        for ref, (_, parts) in zip(piece_refs, pieces):
            for first, is_filter, step, other in parts:
                at = pl.ds(owner_row(step, other, outputs), outputs)
                target = filters if is_filter else grads
                for z in range(target.shape[1] // square):
                    low = first + z * outputs
                    target[at, z * square : (z + 1) * square] = ref[low : low + outputs, :]
        terms = lax.dot_general(
            filters[...], grads[...], (((0,), (0,)), ((), ())), preferred_element_type=F32
        )
        sums = {}
        for tap, (depth_k, row_k, col_k) in enumerate(OFFSETS):
            for z in range(planes):
                key = (2 * z + depth_k, phase_of(row_k, col_k), roll_class(row_k, col_k))
                part = terms[tap * width : (tap + 1) * width, z * square : (z + 1) * square]
                sums[key] = sums[key] + part if key in sums else part
        total = {}
        for (frame, phase, kind), part in sums.items():
            part = shift_cells(part, kind // 2, kind % 2, side)
            key = (frame, phase)
            total[key] = total[key] + part if key in total else part
        for (frame, phase), part in total.items():
            if frame < 0:
                down_ref[phase * width : (phase + 1) * width, :] = part.astype(BF16)
            else:
                out_ref[frame, :, phase * square : (phase + 1) * square] = part
        down_ref[4 * width :, :] = active_ref[:, :square]

    return call(
        kernel,
        (
            jax.ShapeDtypeStruct((2 * planes, width, 4 * square), F32),
            jax.ShapeDtypeStruct((4 * width + outputs, square), BF16),
        ),
        active,
        *[piece for piece, _ in pieces],
        scratch=[
            pltpu.VMEM((devices * outputs, cells), BF16),
            pltpu.VMEM((devices * outputs, 2 * square), BF16),
        ],
    )


def mix_part(low, active, packed, framed_grad, group_filter, side):
    outputs, cells = active.shape
    square = side * side
    planes = cells // square
    taps, width, _ = group_filter.shape
    in_planes, in_chan, _ = framed_grad.shape

    def kernel(low_ref, mid_ref, packed_ref, grad_ref, group_ref, out_ref, sum_ref, windows_ref):
        def store(tap, inner, window):
            windows_ref[
                tap * outputs : (tap + 1) * outputs, inner * square : (inner + 1) * square
            ] = window

        middle = [mid_ref[:, z * square : (z + 1) * square] for z in range(planes)]
        fill_windows([low_ref[...]] + middle + [packed_ref[4 * in_chan :, :]], store, 1, side)
        weights = jnp.concatenate(
            [block_diagonal(group_ref[tap].astype(F32), outputs) for tap in range(taps)], axis=0
        ).astype(BF16)
        mixed = lax.dot_general(
            weights, windows_ref[...], (((0,), (0,)), ((), ())), preferred_element_type=F32
        ).astype(BF16)
        for z in range(planes):
            out_ref[z] = mixed[:, z * square : (z + 1) * square]
        for frame in range(in_planes - 1):
            sum_ref[frame] = grad_ref[frame]
        for phase in range(4):
            at = slice(phase * square, (phase + 1) * square)
            from_above = packed_ref[phase * in_chan : (phase + 1) * in_chan, :].astype(F32)
            sum_ref[in_planes - 1, :, at] = grad_ref[in_planes - 1, :, at] + from_above

    return call(
        kernel,
        (
            jax.ShapeDtypeStruct((planes, outputs, square), BF16),
            jax.ShapeDtypeStruct(framed_grad.shape, F32),
        ),
        low,
        active,
        packed,
        framed_grad,
        group_filter,
        scratch=[pltpu.VMEM((taps * outputs, cells), BF16)],
    )


def sum_part(received, scale):
    devices, rows, lanes = received.shape

    def kernel(src, dst):
        total = src[0].astype(F32)
        for index in range(1, devices):
            total = total + src[index].astype(F32)
        total = total * scale
        total = total.astype(BF16)
        for index in range(devices):
            dst[index] = total

    return call(kernel, jax.ShapeDtypeStruct(received.shape, BF16), received)


def final_part(gathered, taps, outputs, width):
    rows = taps * outputs
    blocks = -(-rows // 128)

    def kernel(src, filter_ref, group_ref):
        filter_ref[...] = src[:rows, :].astype(F32).reshape(taps, outputs, 128)
        tail = src[rows:, :].astype(F32)
        flat = jnp.concatenate(
            [tail[i * width : (i + 1) * width, :] for i in range(blocks)], axis=1
        )
        for tap in range(taps):
            group_ref[tap] = flat[:, tap * outputs : (tap + 1) * outputs]

    return call(
        kernel,
        (
            jax.ShapeDtypeStruct((taps, outputs, 128), F32),
            jax.ShapeDtypeStruct((taps, width, outputs), F32),
        ),
        gathered,
    )


def body(volume, conv_in, conv_group, cotangent):
    in_chan, in_planes, flat_in = volume.shape
    side = math.isqrt(flat_in) // 2
    square = side * side
    planes = in_planes // 2
    cells = planes * square
    taps, outputs, inputs = conv_in.shape
    width = conv_group.shape[2]
    slabs = lax.axis_size("space")
    blocks = lax.axis_size("chan")

    def along_space(block, step):
        return lax.ppermute(block, "space", [(i, (i + step) % slabs) for i in range(slabs)])

    def along_chips(block, step):
        return lax.ppermute(
            block, "chan", [(i, (i + 2 * step) % blocks) for i in range(blocks)]
        )

    def other_core(block):
        return lax.ppermute(block, "chan", [(i, i ^ 1) for i in range(blocks)])

    def joined(*parts):
        return jnp.concatenate(parts, axis=0)

    own, packed, upstream = prep_part(volume, cotangent)
    frame = 4 * in_chan
    packed = along_space(packed, 1)
    up_high = along_space(upstream[:outputs], -1)
    group_filter = jnp.transpose(conv_group, (0, 2, 1))
    act_grad, windows = upstream_part(packed, upstream, up_high, group_filter, side)
    sent = split_filter(conv_in, in_chan, square)

    slots = list(range(4 * (in_planes + 1)))
    length = len(slots) * in_chan
    cut = len(slots) // 2
    own, up_high = lax.optimization_barrier((own, up_high))
    framed = joined(packed[:frame], own)
    from_low = along_chips(framed, 1)
    from_high = along_chips(framed, -1)
    from_low, act_grad, sent = lax.optimization_barrier((from_low, act_grad, sent))
    far_low = along_chips(from_low[: cut * in_chan], 1)
    far_high = along_chips(from_high[cut * in_chan :], -1)
    near_other = other_core(joined(from_low, from_high))
    far_other = other_core(joined(far_low, far_high))
    pieces = [
        (framed, [(0, slots, 0, False)]),
        (other_core(framed), [(0, slots, 0, True)]),
        (from_low, [(0, slots, -1, False)]),
        (from_high, [(0, slots, 1, False)]),
        (near_other, [(0, slots, -1, True), (length, slots, 1, True)]),
        (far_low, [(0, slots[:cut], 2, False)]),
        (far_high, [(0, slots[cut:], 2, False)]),
        (far_other, [(0, slots, 2, True)]),
    ]

    rows = -(-(taps * outputs + 64) // (slabs * 32)) * slabs * 32
    active, hidden_grad, terms = main_part(
        pieces, conv_in, act_grad, windows, width, rows, side
    )
    received = lax.all_to_all(
        terms.reshape(slabs, rows // slabs, 128), "space", split_axis=0, concat_axis=0, tiled=True
    )
    here, up, down, far = sent
    act_low = along_space(active[:, cells - square :], 1)
    up = along_chips(joined(hidden_grad, up), 1)
    down = along_chips(joined(hidden_grad, down), -1)
    far = along_chips(joined(hidden_grad, far), 2)
    block = 2 * outputs
    near = other_core(joined(hidden_grad, here[:block]))
    up, near, act_low = lax.optimization_barrier((up, near, act_low))
    crossed = other_core(
        joined(*[part for ring in (up, down, far) for part in (ring[:block], ring[2 * block :])])
    )
    steps = (-1, 1, 2)
    grads = [
        (hidden_grad, [(0, False, 0, False)]),
        (here, [(block, True, 0, False)]),
        (near, [(0, False, 0, True), (block, True, 0, True)]),
        (crossed, [(i * 2 * block, False, step, True) for i, step in enumerate(steps)]
         + [((2 * i + 1) * block, True, step, True) for i, step in enumerate(steps)]),
    ]
    for ring, step in zip((up, down, far), steps):
        grads.append((ring, [(0, False, step, False), (block, True, step, False)]))
    framed_grad, lowest = input_part(grads, active, in_chan, side)
    received, lowest = lax.optimization_barrier((received, lowest))
    scale = 1.0 / math.sqrt(slabs * cells)
    gathered = lax.all_to_all(
        sum_part(received, scale), "space", split_axis=0, concat_axis=0, tiled=True
    )
    filter_grad, group_grad = final_part(gathered.reshape(rows, 128), taps, outputs, width)

    mixed, input_grad = mix_part(
        act_low, active, along_space(lowest, -1), framed_grad, group_filter, side
    )
    return (
        jnp.transpose(mixed, (1, 0, 2)),
        jnp.transpose(input_grad, (1, 0, 2)),
        filter_grad,
        jnp.transpose(group_grad, (0, 2, 1)),
    )


def solution(mesh):
    return jax.shard_map(
        body,
        mesh=mesh,
        in_specs=(
            P("chan", "space", None),
            P(None, "chan", None),
            P(None, "chan", None),
            P("chan", "space", None),
        ),
        out_specs=(
            P("chan", "space", None),
            P("chan", "space", None),
            P(None, "chan", None),
            P(None, "chan", None),
        ),
        check_vma=False,
    )
```

```python
import math

import jax
import jax.numpy as jnp
from jax import lax
from jax.experimental import pallas as pl
from jax.experimental.pallas import tpu as pltpu
from jax.sharding import PartitionSpec as P

OFFSETS = [
    (first, second, third) for first in (-1, 0, 1) for second in (-1, 0, 1) for third in (-1, 0, 1)
]
TAPS = len(OFFSETS)
BF16 = jnp.bfloat16
F32 = jnp.float32
VMEM_LIMIT = 16 * 1024 * 1024


def phase_of(row_k, col_k):
    return 2 * (row_k != 0) + (col_k != 0)


def roll_class(row_k, col_k):
    return 2 * (row_k < 0) + (col_k < 0)


def shift_cells(plane, row_k, col_k, side):
    square = side * side
    moved = plane
    if col_k:
        inside = pltpu.roll(moved, (-col_k) % square, 1)
        wrapped = pltpu.roll(moved, (col_k * (side - 1)) % square, 1)
        column = lax.broadcasted_iota(jnp.int32, moved.shape, 1) % side
        moved = jnp.where(column == (side - 1 if col_k > 0 else 0), wrapped, inside)
    if row_k:
        moved = pltpu.roll(moved, (-row_k * side) % square, 1)
    return moved


def call(kernel, outs, *args, scratch=(), flops=0, moved=0):
    whole = pl.BlockSpec(memory_space=pltpu.VMEM)
    single = not isinstance(outs, (tuple, list))
    return pl.pallas_call(
        kernel,
        out_shape=outs,
        in_specs=[whole] * len(args),
        out_specs=whole if single else [whole] * len(outs),
        scratch_shapes=list(scratch),
        compiler_params=pltpu.CompilerParams(vmem_limit_bytes=VMEM_LIMIT),
        cost_estimate=pl.CostEstimate(flops=flops, bytes_accessed=moved, transcendentals=0),
    )(*args)


def prep_part(volume, cotangent):
    in_chan, in_planes, flat_in = volume.shape
    outputs, planes, square = cotangent.shape

    def kernel(vol_ref, cot_ref, own_ref, packed_ref, cells_ref):
        for frame in range(in_planes):
            for phase in range(4):
                low = (frame * 4 + phase) * in_chan
                part = vol_ref[frame, :, phase * square : (phase + 1) * square]
                own_ref[low : low + in_chan, :] = part
                if frame == in_planes - 1:
                    packed_ref[phase * in_chan : (phase + 1) * in_chan, :] = part
        for z in range(planes):
            cells_ref[z * outputs : (z + 1) * outputs, :] = cot_ref[z]
        packed_ref[4 * in_chan :, :] = cot_ref[planes - 1]

    return call(
        kernel,
        (
            jax.ShapeDtypeStruct((in_planes * 4 * in_chan, square), BF16),
            jax.ShapeDtypeStruct((4 * in_chan + outputs, square), BF16),
            jax.ShapeDtypeStruct((planes * outputs, square), BF16),
        ),
        jnp.transpose(volume, (1, 0, 2)),
        jnp.transpose(cotangent, (1, 0, 2)),
    )


def split_filter(conv_in, in_chan, square):
    taps, outputs, inputs = conv_in.shape
    count = inputs // in_chan
    block_rows = 2 * outputs
    short = 2 * square - taps * in_chan

    def kernel(conv_ref, here_ref, up_ref, down_ref, far_ref, blocks):
        me = lax.axis_index("chan")
        for owner in range(count):
            steps = lax.rem(owner // 2 + count // 2 - me // 2, count // 2)
            crossed = lax.rem(owner + me, 2)
            wide = [conv_ref[tap, :, owner * in_chan : (owner + 1) * in_chan] for tap in range(taps)]
            wide = jnp.concatenate(wide + [jnp.zeros((outputs, short), BF16)], axis=1)
            blocks[2 * steps + crossed, :outputs, :] = wide[:, :square]
            blocks[2 * steps + crossed, outputs:, :] = wide[:, square:]
        for ref, order in ((here_ref, (1, 0)), (up_ref, (2, 3)), (down_ref, (6, 7)), (far_ref, (4, 5))):
            for index, block in enumerate(order):
                ref[index * block_rows : (index + 1) * block_rows, :] = blocks[block]

    return call(
        kernel,
        [jax.ShapeDtypeStruct((2 * block_rows, square), BF16)] * 4,
        conv_in,
        scratch=[pltpu.VMEM((count, block_rows, square), BF16)],
    )


def fill_windows(planes, store, direction, side):
    count = len(planes) - 2
    for index, plane in enumerate(planes):
        plane = plane.astype(F32)
        for row_k in (-1, 0, 1):
            for col_k in (-1, 0, 1):
                window = shift_cells(plane, direction * row_k, direction * col_k, side).astype(BF16)
                for depth_k in (-1, 0, 1):
                    inner = index - 1 - direction * depth_k
                    if 0 <= inner < count:
                        tap = 9 * (depth_k + 1) + 3 * (row_k + 1) + col_k + 1
                        store(tap, inner, window)


def block_diagonal(values, outputs):
    width, columns = values.shape
    tiled = jnp.concatenate([values] * (outputs // width), axis=0)
    row = lax.broadcasted_iota(jnp.int32, tiled.shape, 0)
    column = lax.broadcasted_iota(jnp.int32, tiled.shape, 1) % outputs
    return jnp.where(row // width == column // width, tiled, jnp.zeros_like(tiled))


def upstream_part(packed, cotangent, high, group_filter, side):
    square = side * side
    taps, width, outputs = group_filter.shape
    planes = cotangent.shape[0] // outputs
    cells = planes * square
    skipped = packed.shape[0] - outputs

    def kernel(low_ref, mid_ref, high_ref, group_ref, grad_ref, windows_ref):
        def store(tap, inner, window):
            windows_ref[
                tap * outputs : (tap + 1) * outputs, inner * square : (inner + 1) * square
            ] = window

        middle = [mid_ref[z * outputs : (z + 1) * outputs, :] for z in range(planes)]
        fill_windows([low_ref[skipped:, :]] + middle + [high_ref[...]], store, -1, side)
        flat = jnp.concatenate([group_ref[tap].astype(F32) for tap in range(taps)], axis=1)
        weights = block_diagonal(flat, outputs).astype(BF16)
        grad_ref[...] = jnp.dot(weights, windows_ref[...], preferred_element_type=F32)

    return call(
        kernel,
        (
            jax.ShapeDtypeStruct((outputs, cells), F32),
            jax.ShapeDtypeStruct((taps * outputs, cells), BF16),
        ),
        packed,
        cotangent,
        high,
        group_filter,
    )


def owner_row(step, other, rows):
    me = lax.axis_index("chan")
    count = lax.axis_size("chan")
    owner = lax.rem(me + (2 * step) % count, count)
    if other:
        owner = owner + 1 - 2 * lax.rem(owner, 2)
    return pl.multiple_of(owner * rows, rows)


def main_part(pieces, conv_in, act_grad, windows, width, rows, side):
    taps, outputs, inputs = conv_in.shape
    square = side * side
    cells = act_grad.shape[1]
    planes = cells // square
    frames = 2 * planes + 1
    depth = 12 * inputs
    in_chan = inputs // lax.axis_size("chan")
    filter_rows = taps * outputs
    group_rows = -(-filter_rows // 128) * width

    def kernel(*refs):
        conv_ref, grad_ref, windows_ref = refs[:3]
        piece_refs = refs[3 : 3 + len(pieces)]
        active_ref, hidden_grad_ref, terms_ref, field, filters = refs[3 + len(pieces) :]
        for ref, (_, parts) in zip(piece_refs, pieces):
            for first, slots, step, other in parts:
                base = owner_row(step, other, in_chan)
                for index, slot in enumerate(slots):
                    low = first + index * in_chan
                    field[pl.ds(slot * inputs + base, in_chan), :] = ref[low : low + in_chan, :]
        filters[...] = jnp.zeros_like(filters)
        places = []
        for tap, (depth_k, row_k, col_k) in enumerate(OFFSETS):
            top = roll_class(row_k, col_k) * outputs
            left = ((depth_k + 1) * 4 + phase_of(row_k, col_k)) * inputs
            places.append((slice(top, top + outputs), slice(left, left + inputs)))
            filters[places[-1]] = conv_ref[tap]
        terms = jnp.zeros((4 * outputs, depth), F32)
        actives = []
        for z in range(planes):
            view = field[8 * inputs * z : 8 * inputs * z + depth, :]
            sums = jnp.dot(filters[...], view, preferred_element_type=F32)
            hidden = sums[:outputs]
            for kind, (row_k, col_k) in ((1, (0, -1)), (2, (-1, 0)), (3, (-1, -1))):
                part = sums[kind * outputs : (kind + 1) * outputs]
                hidden = hidden + shift_cells(part, row_k, col_k, side)
            sigmoid = 1.0 / (1.0 + jnp.exp(-hidden))
            active = (hidden * sigmoid).astype(BF16)
            at = slice(z * square, (z + 1) * square)
            slope = sigmoid * (1.0 + hidden * (1.0 - sigmoid))
            grad = grad_ref[:, at] * slope
            active_ref[:, at] = active
            actives.append(active)
            rounded = grad.astype(BF16)
            hidden_grad_ref[z * outputs : (z + 1) * outputs, :] = rounded
            grad = rounded.astype(F32)
            shifted = jnp.concatenate(
                [shift_cells(grad, row_k, col_k, side) for row_k in (0, 1) for col_k in (0, 1)],
                axis=0,
            ).astype(BF16)
            terms = terms + lax.dot_general(
                shifted, view, (((1,), (1,)), ((), ())), preferred_element_type=F32
            )
        for tap, at in enumerate(places):
            terms_ref[tap * outputs : (tap + 1) * outputs, :] = terms[at].astype(BF16)
        pairs = lax.dot_general(
            jnp.concatenate(actives, axis=1),
            windows_ref[...],
            (((1,), (1,)), ((), ())),
            preferred_element_type=F32,
        )
        group = lax.broadcasted_iota(jnp.int32, (width, filter_rows), 1) % outputs // width
        kept = jnp.zeros((width, filter_rows), F32)
        for index in range(outputs // width):
            block = pairs[index * width : (index + 1) * width]
            kept = kept + jnp.where(group == index, block, 0.0)
        short = group_rows // width * 128 - filter_rows
        kept = jnp.concatenate([kept, jnp.zeros((width, short), F32)], axis=1)
        tail = [kept[:, 128 * i : 128 * (i + 1)] for i in range(group_rows // width)]
        tail.append(jnp.zeros((rows - filter_rows - group_rows, 128), F32))
        terms_ref[filter_rows:, :] = jnp.concatenate(tail, axis=0).astype(BF16)

    return call(
        kernel,
        (
            jax.ShapeDtypeStruct((outputs, cells), BF16),
            jax.ShapeDtypeStruct((planes * outputs, square), BF16),
            jax.ShapeDtypeStruct((rows, 128), BF16),
        ),
        conv_in,
        act_grad,
        windows,
        *[piece for piece, _ in pieces],
        scratch=[
            pltpu.VMEM((frames * 4 * inputs, square), BF16),
            pltpu.VMEM((4 * outputs, depth), BF16),
        ],
    )


def input_part(pieces, active, width, side):
    square = side * side
    outputs, cells = active.shape
    planes = cells // square
    devices = lax.axis_size("chan")

    def kernel(active_ref, *refs):
        piece_refs = refs[: len(pieces)]
        out_ref, down_ref, grads, filters = refs[len(pieces) :]
        for ref, (_, parts) in zip(piece_refs, pieces):
            for first, is_filter, step, other in parts:
                at = pl.ds(owner_row(step, other, outputs), outputs)
                target = filters if is_filter else grads
                for z in range(target.shape[1] // square):
                    low = first + z * outputs
                    target[at, z * square : (z + 1) * square] = ref[low : low + outputs, :]
        terms = lax.dot_general(
            filters[...], grads[...], (((0,), (0,)), ((), ())), preferred_element_type=F32
        )
        sums = {}
        for tap, (depth_k, row_k, col_k) in enumerate(OFFSETS):
            for z in range(planes):
                key = (2 * z + depth_k, phase_of(row_k, col_k), roll_class(row_k, col_k))
                part = terms[tap * width : (tap + 1) * width, z * square : (z + 1) * square]
                sums[key] = sums[key] + part if key in sums else part
        total = {}
        for (frame, phase, kind), part in sums.items():
            part = shift_cells(part, kind // 2, kind % 2, side)
            key = (frame, phase)
            total[key] = total[key] + part if key in total else part
        for (frame, phase), part in total.items():
            if frame < 0:
                down_ref[phase * width : (phase + 1) * width, :] = part.astype(BF16)
            else:
                out_ref[frame, :, phase * square : (phase + 1) * square] = part
        down_ref[4 * width :, :] = active_ref[:, :square]

    return call(
        kernel,
        (
            jax.ShapeDtypeStruct((2 * planes, width, 4 * square), F32),
            jax.ShapeDtypeStruct((4 * width + outputs, square), BF16),
        ),
        active,
        *[piece for piece, _ in pieces],
        scratch=[
            pltpu.VMEM((devices * outputs, cells), BF16),
            pltpu.VMEM((devices * outputs, 2 * square), BF16),
        ],
    )


def mix_part(low, active, packed, framed_grad, group_filter, side):
    outputs, cells = active.shape
    square = side * side
    planes = cells // square
    taps, width, _ = group_filter.shape
    in_planes, in_chan, _ = framed_grad.shape

    def kernel(low_ref, mid_ref, packed_ref, grad_ref, group_ref, out_ref, sum_ref, windows_ref):
        def store(tap, inner, window):
            windows_ref[
                tap * outputs : (tap + 1) * outputs, inner * square : (inner + 1) * square
            ] = window

        middle = [mid_ref[:, z * square : (z + 1) * square] for z in range(planes)]
        fill_windows([low_ref[...]] + middle + [packed_ref[4 * in_chan :, :]], store, 1, side)
        weights = jnp.concatenate(
            [block_diagonal(group_ref[tap].astype(F32), outputs) for tap in range(taps)], axis=0
        ).astype(BF16)
        mixed = lax.dot_general(
            weights, windows_ref[...], (((0,), (0,)), ((), ())), preferred_element_type=F32
        ).astype(BF16)
        for z in range(planes):
            out_ref[:, z, :] = mixed[:, z * square : (z + 1) * square]
        for frame in range(in_planes - 1):
            sum_ref[:, frame, :] = grad_ref[frame]
        for phase in range(4):
            at = slice(phase * square, (phase + 1) * square)
            from_above = packed_ref[phase * in_chan : (phase + 1) * in_chan, :].astype(F32)
            sum_ref[:, in_planes - 1, at] = grad_ref[in_planes - 1, :, at] + from_above

    return call(
        kernel,
        (
            jax.ShapeDtypeStruct((outputs, planes, square), BF16),
            jax.ShapeDtypeStruct((in_chan, in_planes, 4 * square), F32),
        ),
        low,
        active,
        packed,
        framed_grad,
        group_filter,
        scratch=[pltpu.VMEM((taps * outputs, cells), BF16)],
    )


def sum_part(received, scale):
    devices, rows, lanes = received.shape

    def kernel(src, dst):
        total = src[0].astype(F32)
        for index in range(1, devices):
            total = total + src[index].astype(F32)
        total = total * scale
        total = total.astype(BF16)
        for index in range(devices):
            dst[index] = total

    return call(kernel, jax.ShapeDtypeStruct(received.shape, BF16), received)


def final_part(gathered, taps, outputs, width):
    rows = taps * outputs
    blocks = -(-rows // 128)

    def kernel(src, filter_ref, group_ref):
        filter_ref[...] = src[:rows, :].astype(F32).reshape(taps, outputs, 128)
        tail = src[rows:, :].astype(F32)
        flat = jnp.concatenate(
            [tail[i * width : (i + 1) * width, :] for i in range(blocks)], axis=1
        )
        for tap in range(taps):
            group_ref[tap] = flat[:, tap * outputs : (tap + 1) * outputs]

    return call(
        kernel,
        (
            jax.ShapeDtypeStruct((taps, outputs, 128), F32),
            jax.ShapeDtypeStruct((taps, width, outputs), F32),
        ),
        gathered,
    )


def body(volume, conv_in, conv_group, cotangent):
    in_chan, in_planes, flat_in = volume.shape
    side = math.isqrt(flat_in) // 2
    square = side * side
    planes = in_planes // 2
    cells = planes * square
    taps, outputs, inputs = conv_in.shape
    width = conv_group.shape[2]
    slabs = lax.axis_size("space")
    blocks = lax.axis_size("chan")

    def along_space(block, step):
        return lax.ppermute(block, "space", [(i, (i + step) % slabs) for i in range(slabs)])

    def along_chips(block, step):
        return lax.ppermute(
            block, "chan", [(i, (i + 2 * step) % blocks) for i in range(blocks)]
        )

    def other_core(block):
        return lax.ppermute(block, "chan", [(i, i ^ 1) for i in range(blocks)])

    def joined(*parts):
        return jnp.concatenate(parts, axis=0)

    own, packed, upstream = prep_part(volume, cotangent)
    frame = 4 * in_chan
    packed = along_space(packed, 1)
    up_high = along_space(upstream[:outputs], -1)
    group_filter = jnp.transpose(conv_group, (0, 2, 1))
    act_grad, windows = upstream_part(packed, upstream, up_high, group_filter, side)
    sent = split_filter(conv_in, in_chan, square)

    slots = list(range(4 * (in_planes + 1)))
    length = len(slots) * in_chan
    cut = len(slots) // 2
    own, up_high = lax.optimization_barrier((own, up_high))
    framed = joined(packed[:frame], own)
    from_low = along_chips(framed, 1)
    from_high = along_chips(framed, -1)
    from_low, act_grad, sent = lax.optimization_barrier((from_low, act_grad, sent))
    far_low = along_chips(from_low[: cut * in_chan], 1)
    far_high = along_chips(from_high[cut * in_chan :], -1)
    near_other = other_core(joined(from_low, from_high))
    far_other = other_core(joined(far_low, far_high))
    pieces = [
        (framed, [(0, slots, 0, False)]),
        (other_core(framed), [(0, slots, 0, True)]),
        (from_low, [(0, slots, -1, False)]),
        (from_high, [(0, slots, 1, False)]),
        (near_other, [(0, slots, -1, True), (length, slots, 1, True)]),
        (far_low, [(0, slots[:cut], 2, False)]),
        (far_high, [(0, slots[cut:], 2, False)]),
        (far_other, [(0, slots, 2, True)]),
    ]

    rows = -(-(taps * outputs + 64) // (slabs * 32)) * slabs * 32
    active, hidden_grad, terms = main_part(
        pieces, conv_in, act_grad, windows, width, rows, side
    )
    received = lax.all_to_all(
        terms.reshape(slabs, rows // slabs, 128), "space", split_axis=0, concat_axis=0, tiled=True
    )
    here, up, down, far = sent
    act_low = along_space(active[:, cells - square :], 1)
    up = along_chips(joined(hidden_grad, up), 1)
    down = along_chips(joined(hidden_grad, down), -1)
    far = along_chips(joined(hidden_grad, far), 2)
    block = 2 * outputs
    near = other_core(joined(hidden_grad, here[:block]))
    up, near = lax.optimization_barrier((up, near))
    crossed = other_core(
        joined(*[part for ring in (up, down, far) for part in (ring[:block], ring[2 * block :])])
    )
    steps = (-1, 1, 2)
    grads = [
        (hidden_grad, [(0, False, 0, False)]),
        (here, [(block, True, 0, False)]),
        (near, [(0, False, 0, True), (block, True, 0, True)]),
        (crossed, [(i * 2 * block, False, step, True) for i, step in enumerate(steps)]
         + [((2 * i + 1) * block, True, step, True) for i, step in enumerate(steps)]),
    ]
    for ring, step in zip((up, down, far), steps):
        grads.append((ring, [(0, False, step, False), (block, True, step, False)]))
    framed_grad, lowest = input_part(grads, active, in_chan, side)
    received, lowest, act_low = lax.optimization_barrier((received, lowest, act_low))
    scale = 1.0 / math.sqrt(slabs * cells)
    gathered = lax.all_to_all(
        sum_part(received, scale), "space", split_axis=0, concat_axis=0, tiled=True
    )
    filter_grad, group_grad = final_part(gathered.reshape(rows, 128), taps, outputs, width)

    mixed, input_grad = mix_part(
        act_low, active, along_space(lowest, -1), framed_grad, group_filter, side
    )
    return (
        mixed,
        input_grad,
        filter_grad,
        jnp.transpose(group_grad, (0, 2, 1)),
    )


def solution(mesh):
    return jax.shard_map(
        body,
        mesh=mesh,
        in_specs=(
            P("chan", "space", None),
            P(None, "chan", None),
            P(None, "chan", None),
            P("chan", "space", None),
        ),
        out_specs=(
            P("chan", "space", None),
            P("chan", "space", None),
            P(None, "chan", None),
            P(None, "chan", None),
        ),
        check_vma=False,
    )
```

```python
import math

import jax
import jax.numpy as jnp
from jax import lax
from jax.experimental import pallas as pl
from jax.experimental.pallas import tpu as pltpu
from jax.sharding import PartitionSpec as P

OFFSETS = [
    (first, second, third) for first in (-1, 0, 1) for second in (-1, 0, 1) for third in (-1, 0, 1)
]
TAPS = len(OFFSETS)
BF16 = jnp.bfloat16
F32 = jnp.float32
VMEM_LIMIT = 16 * 1024 * 1024


def phase_of(row_k, col_k):
    return 2 * (row_k != 0) + (col_k != 0)


def roll_class(row_k, col_k):
    return 2 * (row_k < 0) + (col_k < 0)


def shift_cells(plane, row_k, col_k, side):
    square = side * side
    moved = plane
    if col_k:
        inside = pltpu.roll(moved, (-col_k) % square, 1)
        wrapped = pltpu.roll(moved, (col_k * (side - 1)) % square, 1)
        column = lax.broadcasted_iota(jnp.int32, moved.shape, 1) % side
        moved = jnp.where(column == (side - 1 if col_k > 0 else 0), wrapped, inside)
    if row_k:
        moved = pltpu.roll(moved, (-row_k * side) % square, 1)
    return moved


def call(kernel, outs, *args, scratch=(), flops=0, moved=0):
    whole = pl.BlockSpec(memory_space=pltpu.VMEM)
    single = not isinstance(outs, (tuple, list))
    return pl.pallas_call(
        kernel,
        out_shape=outs,
        in_specs=[whole] * len(args),
        out_specs=whole if single else [whole] * len(outs),
        scratch_shapes=list(scratch),
        compiler_params=pltpu.CompilerParams(vmem_limit_bytes=VMEM_LIMIT),
        cost_estimate=pl.CostEstimate(flops=flops, bytes_accessed=moved, transcendentals=0),
    )(*args)


def prep_part(volume, cotangent):
    in_chan, in_planes, flat_in = volume.shape
    outputs, planes, square = cotangent.shape

    def kernel(vol_ref, cot_ref, own_ref, packed_ref, cells_ref):
        for frame in range(in_planes):
            for phase in range(4):
                low = (frame * 4 + phase) * in_chan
                part = vol_ref[frame, :, phase * square : (phase + 1) * square]
                own_ref[low : low + in_chan, :] = part
                if frame == in_planes - 1:
                    packed_ref[phase * in_chan : (phase + 1) * in_chan, :] = part
        for z in range(planes):
            cells_ref[z * outputs : (z + 1) * outputs, :] = cot_ref[z]
        packed_ref[4 * in_chan :, :] = cot_ref[planes - 1]

    return call(
        kernel,
        (
            jax.ShapeDtypeStruct((in_planes * 4 * in_chan, square), BF16),
            jax.ShapeDtypeStruct((4 * in_chan + outputs, square), BF16),
            jax.ShapeDtypeStruct((planes * outputs, square), BF16),
        ),
        jnp.transpose(volume, (1, 0, 2)),
        jnp.transpose(cotangent, (1, 0, 2)),
    )


def split_filter(conv_in, in_chan, square):
    taps, outputs, inputs = conv_in.shape
    count = inputs // in_chan
    block_rows = 2 * outputs
    short = 2 * square - taps * in_chan

    def kernel(conv_ref, here_ref, up_ref, down_ref, far_ref, blocks):
        me = lax.axis_index("chan")
        for owner in range(count):
            steps = lax.rem(owner // 2 + count // 2 - me // 2, count // 2)
            crossed = lax.rem(owner + me, 2)
            wide = [conv_ref[tap, :, owner * in_chan : (owner + 1) * in_chan] for tap in range(taps)]
            wide = jnp.concatenate(wide + [jnp.zeros((outputs, short), BF16)], axis=1)
            blocks[2 * steps + crossed, :outputs, :] = wide[:, :square]
            blocks[2 * steps + crossed, outputs:, :] = wide[:, square:]
        for ref, order in ((here_ref, (1, 0)), (up_ref, (2, 3)), (down_ref, (6, 7)), (far_ref, (4, 5))):
            for index, block in enumerate(order):
                ref[index * block_rows : (index + 1) * block_rows, :] = blocks[block]

    return call(
        kernel,
        [jax.ShapeDtypeStruct((2 * block_rows, square), BF16)] * 4,
        conv_in,
        scratch=[pltpu.VMEM((count, block_rows, square), BF16)],
    )


def fill_windows(planes, store, direction, side):
    count = len(planes) - 2
    for index, plane in enumerate(planes):
        plane = plane.astype(F32)
        for row_k in (-1, 0, 1):
            for col_k in (-1, 0, 1):
                window = shift_cells(plane, direction * row_k, direction * col_k, side).astype(BF16)
                for depth_k in (-1, 0, 1):
                    inner = index - 1 - direction * depth_k
                    if 0 <= inner < count:
                        tap = 9 * (depth_k + 1) + 3 * (row_k + 1) + col_k + 1
                        store(tap, inner, window)


def block_diagonal(values, outputs):
    width, columns = values.shape
    tiled = jnp.concatenate([values] * (outputs // width), axis=0)
    row = lax.broadcasted_iota(jnp.int32, tiled.shape, 0)
    column = lax.broadcasted_iota(jnp.int32, tiled.shape, 1) % outputs
    return jnp.where(row // width == column // width, tiled, jnp.zeros_like(tiled))


def upstream_part(packed, cotangent, high, group_filter, side):
    square = side * side
    taps, width, outputs = group_filter.shape
    planes = cotangent.shape[0] // outputs
    cells = planes * square
    skipped = packed.shape[0] - outputs

    def kernel(low_ref, mid_ref, high_ref, group_ref, grad_ref, windows_ref):
        def store(tap, inner, window):
            windows_ref[
                tap * outputs : (tap + 1) * outputs, inner * square : (inner + 1) * square
            ] = window

        middle = [mid_ref[z * outputs : (z + 1) * outputs, :] for z in range(planes)]
        fill_windows([low_ref[skipped:, :]] + middle + [high_ref[...]], store, -1, side)
        flat = jnp.concatenate([group_ref[tap].astype(F32) for tap in range(taps)], axis=1)
        weights = block_diagonal(flat, outputs).astype(BF16)
        grad_ref[...] = jnp.dot(weights, windows_ref[...], preferred_element_type=F32)

    return call(
        kernel,
        (
            jax.ShapeDtypeStruct((outputs, cells), F32),
            jax.ShapeDtypeStruct((taps * outputs, cells), BF16),
        ),
        packed,
        cotangent,
        high,
        group_filter,
        flops=10**10,
    )


def owner_row(step, other, rows):
    me = lax.axis_index("chan")
    count = lax.axis_size("chan")
    owner = lax.rem(me + (2 * step) % count, count)
    if other:
        owner = owner + 1 - 2 * lax.rem(owner, 2)
    return pl.multiple_of(owner * rows, rows)


def main_part(pieces, conv_in, act_grad, windows, width, rows, side):
    taps, outputs, inputs = conv_in.shape
    square = side * side
    cells = act_grad.shape[1]
    planes = cells // square
    frames = 2 * planes + 1
    depth = 12 * inputs
    in_chan = inputs // lax.axis_size("chan")
    filter_rows = taps * outputs
    group_rows = -(-filter_rows // 128) * width

    def kernel(*refs):
        conv_ref, grad_ref, windows_ref = refs[:3]
        piece_refs = refs[3 : 3 + len(pieces)]
        active_ref, hidden_grad_ref, terms_ref, field, filters = refs[3 + len(pieces) :]
        for ref, (_, parts) in zip(piece_refs, pieces):
            for first, slots, step, other in parts:
                base = owner_row(step, other, in_chan)
                for index, slot in enumerate(slots):
                    low = first + index * in_chan
                    field[pl.ds(slot * inputs + base, in_chan), :] = ref[low : low + in_chan, :]
        filters[...] = jnp.zeros_like(filters)
        places = []
        for tap, (depth_k, row_k, col_k) in enumerate(OFFSETS):
            top = roll_class(row_k, col_k) * outputs
            left = ((depth_k + 1) * 4 + phase_of(row_k, col_k)) * inputs
            places.append((slice(top, top + outputs), slice(left, left + inputs)))
            filters[places[-1]] = conv_ref[tap]
        terms = jnp.zeros((4 * outputs, depth), F32)
        actives = []
        for z in range(planes):
            view = field[8 * inputs * z : 8 * inputs * z + depth, :]
            sums = jnp.dot(filters[...], view, preferred_element_type=F32)
            hidden = sums[:outputs]
            for kind, (row_k, col_k) in ((1, (0, -1)), (2, (-1, 0)), (3, (-1, -1))):
                part = sums[kind * outputs : (kind + 1) * outputs]
                hidden = hidden + shift_cells(part, row_k, col_k, side)
            sigmoid = 1.0 / (1.0 + jnp.exp(-hidden))
            active = (hidden * sigmoid).astype(BF16)
            at = slice(z * square, (z + 1) * square)
            slope = sigmoid * (1.0 + hidden * (1.0 - sigmoid))
            grad = grad_ref[:, at] * slope
            active_ref[:, at] = active
            actives.append(active)
            rounded = grad.astype(BF16)
            hidden_grad_ref[z * outputs : (z + 1) * outputs, :] = rounded
            grad = rounded.astype(F32)
            shifted = jnp.concatenate(
                [shift_cells(grad, row_k, col_k, side) for row_k in (0, 1) for col_k in (0, 1)],
                axis=0,
            ).astype(BF16)
            terms = terms + lax.dot_general(
                shifted, view, (((1,), (1,)), ((), ())), preferred_element_type=F32
            )
        for tap, at in enumerate(places):
            terms_ref[tap * outputs : (tap + 1) * outputs, :] = terms[at].astype(BF16)
        pairs = lax.dot_general(
            jnp.concatenate(actives, axis=1),
            windows_ref[...],
            (((1,), (1,)), ((), ())),
            preferred_element_type=F32,
        )
        group = lax.broadcasted_iota(jnp.int32, (width, filter_rows), 1) % outputs // width
        kept = jnp.zeros((width, filter_rows), F32)
        for index in range(outputs // width):
            block = pairs[index * width : (index + 1) * width]
            kept = kept + jnp.where(group == index, block, 0.0)
        short = group_rows // width * 128 - filter_rows
        kept = jnp.concatenate([kept, jnp.zeros((width, short), F32)], axis=1)
        tail = [kept[:, 128 * i : 128 * (i + 1)] for i in range(group_rows // width)]
        tail.append(jnp.zeros((rows - filter_rows - group_rows, 128), F32))
        terms_ref[filter_rows:, :] = jnp.concatenate(tail, axis=0).astype(BF16)

    return call(
        kernel,
        (
            jax.ShapeDtypeStruct((outputs, cells), BF16),
            jax.ShapeDtypeStruct((planes * outputs, square), BF16),
            jax.ShapeDtypeStruct((rows, 128), BF16),
        ),
        conv_in,
        act_grad,
        windows,
        *[piece for piece, _ in pieces],
        scratch=[
            pltpu.VMEM((frames * 4 * inputs, square), BF16),
            pltpu.VMEM((4 * outputs, depth), BF16),
        ],
    )


def input_part(pieces, active, width, side):
    square = side * side
    outputs, cells = active.shape
    planes = cells // square
    devices = lax.axis_size("chan")

    def kernel(active_ref, *refs):
        piece_refs = refs[: len(pieces)]
        out_ref, down_ref, grads, filters = refs[len(pieces) :]
        for ref, (_, parts) in zip(piece_refs, pieces):
            for first, is_filter, step, other in parts:
                at = pl.ds(owner_row(step, other, outputs), outputs)
                target = filters if is_filter else grads
                for z in range(target.shape[1] // square):
                    low = first + z * outputs
                    target[at, z * square : (z + 1) * square] = ref[low : low + outputs, :]
        terms = lax.dot_general(
            filters[...], grads[...], (((0,), (0,)), ((), ())), preferred_element_type=F32
        )
        sums = {}
        for tap, (depth_k, row_k, col_k) in enumerate(OFFSETS):
            for z in range(planes):
                key = (2 * z + depth_k, phase_of(row_k, col_k), roll_class(row_k, col_k))
                part = terms[tap * width : (tap + 1) * width, z * square : (z + 1) * square]
                sums[key] = sums[key] + part if key in sums else part
        total = {}
        for (frame, phase, kind), part in sums.items():
            part = shift_cells(part, kind // 2, kind % 2, side)
            key = (frame, phase)
            total[key] = total[key] + part if key in total else part
        for (frame, phase), part in total.items():
            if frame < 0:
                down_ref[phase * width : (phase + 1) * width, :] = part.astype(BF16)
            else:
                out_ref[frame, :, phase * square : (phase + 1) * square] = part
        down_ref[4 * width :, :] = active_ref[:, :square]

    return call(
        kernel,
        (
            jax.ShapeDtypeStruct((2 * planes, width, 4 * square), F32),
            jax.ShapeDtypeStruct((4 * width + outputs, square), BF16),
        ),
        active,
        *[piece for piece, _ in pieces],
        scratch=[
            pltpu.VMEM((devices * outputs, cells), BF16),
            pltpu.VMEM((devices * outputs, 2 * square), BF16),
        ],
    )


def mix_part(low, active, packed, framed_grad, group_filter, side):
    outputs, cells = active.shape
    square = side * side
    planes = cells // square
    taps, width, _ = group_filter.shape
    in_planes, in_chan, _ = framed_grad.shape

    def kernel(low_ref, mid_ref, packed_ref, grad_ref, group_ref, out_ref, sum_ref, windows_ref):
        def store(tap, inner, window):
            windows_ref[
                tap * outputs : (tap + 1) * outputs, inner * square : (inner + 1) * square
            ] = window

        middle = [mid_ref[:, z * square : (z + 1) * square] for z in range(planes)]
        fill_windows([low_ref[...]] + middle + [packed_ref[4 * in_chan :, :]], store, 1, side)
        weights = jnp.concatenate(
            [block_diagonal(group_ref[tap].astype(F32), outputs) for tap in range(taps)], axis=0
        ).astype(BF16)
        mixed = lax.dot_general(
            weights, windows_ref[...], (((0,), (0,)), ((), ())), preferred_element_type=F32
        ).astype(BF16)
        for z in range(planes):
            out_ref[:, z, :] = mixed[:, z * square : (z + 1) * square]
        for frame in range(in_planes - 1):
            sum_ref[:, frame, :] = grad_ref[frame]
        for phase in range(4):
            at = slice(phase * square, (phase + 1) * square)
            from_above = packed_ref[phase * in_chan : (phase + 1) * in_chan, :].astype(F32)
            sum_ref[:, in_planes - 1, at] = grad_ref[in_planes - 1, :, at] + from_above

    return call(
        kernel,
        (
            jax.ShapeDtypeStruct((outputs, planes, square), BF16),
            jax.ShapeDtypeStruct((in_chan, in_planes, 4 * square), F32),
        ),
        low,
        active,
        packed,
        framed_grad,
        group_filter,
        scratch=[pltpu.VMEM((taps * outputs, cells), BF16)],
    )


def sum_part(received, scale):
    devices, rows, lanes = received.shape

    def kernel(src, dst):
        total = src[0].astype(F32)
        for index in range(1, devices):
            total = total + src[index].astype(F32)
        total = total * scale
        total = total.astype(BF16)
        for index in range(devices):
            dst[index] = total

    return call(kernel, jax.ShapeDtypeStruct(received.shape, BF16), received)


def final_part(gathered, taps, outputs, width):
    rows = taps * outputs
    blocks = -(-rows // 128)

    def kernel(src, filter_ref, group_ref):
        filter_ref[...] = src[:rows, :].astype(F32).reshape(taps, outputs, 128)
        tail = src[rows:, :].astype(F32)
        flat = jnp.concatenate(
            [tail[i * width : (i + 1) * width, :] for i in range(blocks)], axis=1
        )
        for tap in range(taps):
            group_ref[tap] = flat[:, tap * outputs : (tap + 1) * outputs]

    return call(
        kernel,
        (
            jax.ShapeDtypeStruct((taps, outputs, 128), F32),
            jax.ShapeDtypeStruct((taps, width, outputs), F32),
        ),
        gathered,
    )


def body(volume, conv_in, conv_group, cotangent):
    in_chan, in_planes, flat_in = volume.shape
    side = math.isqrt(flat_in) // 2
    square = side * side
    planes = in_planes // 2
    cells = planes * square
    taps, outputs, inputs = conv_in.shape
    width = conv_group.shape[2]
    slabs = lax.axis_size("space")
    blocks = lax.axis_size("chan")

    def along_space(block, step):
        return lax.ppermute(block, "space", [(i, (i + step) % slabs) for i in range(slabs)])

    def along_chips(block, step):
        return lax.ppermute(
            block, "chan", [(i, (i + 2 * step) % blocks) for i in range(blocks)]
        )

    def other_core(block):
        return lax.ppermute(block, "chan", [(i, i ^ 1) for i in range(blocks)])

    def joined(*parts):
        return jnp.concatenate(parts, axis=0)

    own, packed, upstream = prep_part(volume, cotangent)
    frame = 4 * in_chan
    packed = along_space(packed, 1)
    up_high = along_space(upstream[:outputs], -1)
    group_filter = jnp.transpose(conv_group, (0, 2, 1))
    act_grad, windows = upstream_part(packed, upstream, up_high, group_filter, side)
    sent = split_filter(conv_in, in_chan, square)

    slots = list(range(4 * (in_planes + 1)))
    length = len(slots) * in_chan
    cut = len(slots) // 2
    framed = joined(packed[:frame], own)
    from_low = along_chips(framed, 1)
    from_high = along_chips(framed, -1)
    from_low, sent = lax.optimization_barrier((from_low, sent))
    far_low = along_chips(from_low[: cut * in_chan], 1)
    far_high = along_chips(from_high[cut * in_chan :], -1)
    near_other = other_core(joined(from_low, from_high))
    far_other = other_core(joined(far_low, far_high))
    pieces = [
        (framed, [(0, slots, 0, False)]),
        (other_core(framed), [(0, slots, 0, True)]),
        (from_low, [(0, slots, -1, False)]),
        (from_high, [(0, slots, 1, False)]),
        (near_other, [(0, slots, -1, True), (length, slots, 1, True)]),
        (far_low, [(0, slots[:cut], 2, False)]),
        (far_high, [(0, slots[cut:], 2, False)]),
        (far_other, [(0, slots, 2, True)]),
    ]

    rows = -(-(taps * outputs + 64) // (slabs * 32)) * slabs * 32
    active, hidden_grad, terms = main_part(
        pieces, conv_in, act_grad, windows, width, rows, side
    )
    received = lax.all_to_all(
        terms.reshape(slabs, rows // slabs, 128), "space", split_axis=0, concat_axis=0, tiled=True
    )
    here, up, down, far = sent
    act_low = along_space(active[:, cells - square :], 1)
    up = along_chips(joined(hidden_grad, up), 1)
    down = along_chips(joined(hidden_grad, down), -1)
    far = along_chips(joined(hidden_grad, far), 2)
    block = 2 * outputs
    near = other_core(joined(hidden_grad, here[:block]))
    up, near = lax.optimization_barrier((up, near))
    crossed = other_core(
        joined(*[part for ring in (up, down, far) for part in (ring[:block], ring[2 * block :])])
    )
    steps = (-1, 1, 2)
    grads = [
        (hidden_grad, [(0, False, 0, False)]),
        (here, [(block, True, 0, False)]),
        (near, [(0, False, 0, True), (block, True, 0, True)]),
        (crossed, [(i * 2 * block, False, step, True) for i, step in enumerate(steps)]
         + [((2 * i + 1) * block, True, step, True) for i, step in enumerate(steps)]),
    ]
    for ring, step in zip((up, down, far), steps):
        grads.append((ring, [(0, False, step, False), (block, True, step, False)]))
    framed_grad, lowest = input_part(grads, active, in_chan, side)
    received, lowest, act_low = lax.optimization_barrier((received, lowest, act_low))
    scale = 1.0 / math.sqrt(slabs * cells)
    gathered = lax.all_to_all(
        sum_part(received, scale), "space", split_axis=0, concat_axis=0, tiled=True
    )
    filter_grad, group_grad = final_part(gathered.reshape(rows, 128), taps, outputs, width)

    mixed, input_grad = mix_part(
        act_low, active, along_space(lowest, -1), framed_grad, group_filter, side
    )
    return (
        mixed,
        input_grad,
        filter_grad,
        jnp.transpose(group_grad, (0, 2, 1)),
    )


def solution(mesh):
    return jax.shard_map(
        body,
        mesh=mesh,
        in_specs=(
            P("chan", "space", None),
            P(None, "chan", None),
            P(None, "chan", None),
            P("chan", "space", None),
        ),
        out_specs=(
            P("chan", "space", None),
            P("chan", "space", None),
            P(None, "chan", None),
            P(None, "chan", None),
        ),
        check_vma=False,
    )
```

```python
import math

import jax
import jax.numpy as jnp
from jax import lax
from jax.experimental import pallas as pl
from jax.experimental.pallas import tpu as pltpu
from jax.sharding import PartitionSpec as P

OFFSETS = [
    (first, second, third) for first in (-1, 0, 1) for second in (-1, 0, 1) for third in (-1, 0, 1)
]
TAPS = len(OFFSETS)
BF16 = jnp.bfloat16
F32 = jnp.float32
VMEM_LIMIT = 16 * 1024 * 1024


def phase_of(row_k, col_k):
    return 2 * (row_k != 0) + (col_k != 0)


def roll_class(row_k, col_k):
    return 2 * (row_k < 0) + (col_k < 0)


def shift_cells(plane, row_k, col_k, side):
    square = side * side
    moved = plane
    if col_k:
        inside = pltpu.roll(moved, (-col_k) % square, 1)
        wrapped = pltpu.roll(moved, (col_k * (side - 1)) % square, 1)
        column = lax.broadcasted_iota(jnp.int32, moved.shape, 1) % side
        moved = jnp.where(column == (side - 1 if col_k > 0 else 0), wrapped, inside)
    if row_k:
        moved = pltpu.roll(moved, (-row_k * side) % square, 1)
    return moved


def call(kernel, outs, *args, scratch=(), flops=0, moved=0):
    whole = pl.BlockSpec(memory_space=pltpu.VMEM)
    single = not isinstance(outs, (tuple, list))
    return pl.pallas_call(
        kernel,
        out_shape=outs,
        in_specs=[whole] * len(args),
        out_specs=whole if single else [whole] * len(outs),
        scratch_shapes=list(scratch),
        compiler_params=pltpu.CompilerParams(vmem_limit_bytes=VMEM_LIMIT),
        cost_estimate=pl.CostEstimate(flops=flops, bytes_accessed=moved, transcendentals=0),
    )(*args)


def prep_part(volume, cotangent):
    in_chan, in_planes, flat_in = volume.shape
    outputs, planes, square = cotangent.shape

    def kernel(vol_ref, cot_ref, own_ref, packed_ref, cells_ref):
        for frame in range(in_planes):
            for phase in range(4):
                low = (frame * 4 + phase) * in_chan
                part = vol_ref[frame, :, phase * square : (phase + 1) * square]
                own_ref[low : low + in_chan, :] = part
                if frame == in_planes - 1:
                    packed_ref[phase * in_chan : (phase + 1) * in_chan, :] = part
        for z in range(planes):
            cells_ref[z * outputs : (z + 1) * outputs, :] = cot_ref[z]
        packed_ref[4 * in_chan :, :] = cot_ref[planes - 1]

    return call(
        kernel,
        (
            jax.ShapeDtypeStruct((in_planes * 4 * in_chan, square), BF16),
            jax.ShapeDtypeStruct((4 * in_chan + outputs, square), BF16),
            jax.ShapeDtypeStruct((planes * outputs, square), BF16),
        ),
        jnp.transpose(volume, (1, 0, 2)),
        jnp.transpose(cotangent, (1, 0, 2)),
    )


def split_filter(conv_in, in_chan, square):
    taps, outputs, inputs = conv_in.shape
    count = inputs // in_chan
    block_rows = 2 * outputs
    short = 2 * square - taps * in_chan

    def kernel(conv_ref, here_ref, up_ref, down_ref, far_ref, blocks):
        me = lax.axis_index("chan")
        for owner in range(count):
            steps = lax.rem(owner // 2 + count // 2 - me // 2, count // 2)
            crossed = lax.rem(owner + me, 2)
            wide = [conv_ref[tap, :, owner * in_chan : (owner + 1) * in_chan] for tap in range(taps)]
            wide = jnp.concatenate(wide + [jnp.zeros((outputs, short), BF16)], axis=1)
            blocks[2 * steps + crossed, :outputs, :] = wide[:, :square]
            blocks[2 * steps + crossed, outputs:, :] = wide[:, square:]
        for ref, order in ((here_ref, (1, 0)), (up_ref, (2, 3)), (down_ref, (6, 7)), (far_ref, (4, 5))):
            for index, block in enumerate(order):
                ref[index * block_rows : (index + 1) * block_rows, :] = blocks[block]

    return call(
        kernel,
        [jax.ShapeDtypeStruct((2 * block_rows, square), BF16)] * 4,
        conv_in,
        scratch=[pltpu.VMEM((count, block_rows, square), BF16)],
    )


def fill_windows(planes, store, direction, side):
    count = len(planes) - 2
    for index, plane in enumerate(planes):
        plane = plane.astype(F32)
        for row_k in (-1, 0, 1):
            for col_k in (-1, 0, 1):
                window = shift_cells(plane, direction * row_k, direction * col_k, side).astype(BF16)
                for depth_k in (-1, 0, 1):
                    inner = index - 1 - direction * depth_k
                    if 0 <= inner < count:
                        tap = 9 * (depth_k + 1) + 3 * (row_k + 1) + col_k + 1
                        store(tap, inner, window)


def block_diagonal(values, outputs):
    width, columns = values.shape
    tiled = jnp.concatenate([values] * (outputs // width), axis=0)
    row = lax.broadcasted_iota(jnp.int32, tiled.shape, 0)
    column = lax.broadcasted_iota(jnp.int32, tiled.shape, 1) % outputs
    return jnp.where(row // width == column // width, tiled, jnp.zeros_like(tiled))


def upstream_part(packed, cotangent, high, group_filter, side):
    square = side * side
    taps, width, outputs = group_filter.shape
    planes = cotangent.shape[0] // outputs
    cells = planes * square
    skipped = packed.shape[0] - outputs

    def kernel(low_ref, mid_ref, high_ref, group_ref, grad_ref, windows_ref):
        def store(tap, inner, window):
            windows_ref[
                tap * outputs : (tap + 1) * outputs, inner * square : (inner + 1) * square
            ] = window

        middle = [mid_ref[z * outputs : (z + 1) * outputs, :] for z in range(planes)]
        fill_windows([low_ref[skipped:, :]] + middle + [high_ref[...]], store, -1, side)
        flat = jnp.concatenate([group_ref[tap].astype(F32) for tap in range(taps)], axis=1)
        weights = block_diagonal(flat, outputs).astype(BF16)
        grad_ref[...] = jnp.dot(weights, windows_ref[...], preferred_element_type=F32)

    return call(
        kernel,
        (
            jax.ShapeDtypeStruct((outputs, cells), F32),
            jax.ShapeDtypeStruct((taps * outputs, cells), BF16),
        ),
        packed,
        cotangent,
        high,
        group_filter,
        flops=10**10,
    )


def owner_row(step, other, rows):
    me = lax.axis_index("chan")
    count = lax.axis_size("chan")
    owner = lax.rem(me + (2 * step) % count, count)
    if other:
        owner = owner + 1 - 2 * lax.rem(owner, 2)
    return pl.multiple_of(owner * rows, rows)


def main_part(pieces, conv_in, act_grad, windows, width, rows, side):
    taps, outputs, inputs = conv_in.shape
    square = side * side
    cells = act_grad.shape[1]
    planes = cells // square
    frames = 2 * planes + 1
    depth = 12 * inputs
    in_chan = inputs // lax.axis_size("chan")
    filter_rows = taps * outputs
    group_rows = -(-filter_rows // 128) * width

    def kernel(*refs):
        conv_ref, grad_ref, windows_ref = refs[:3]
        piece_refs = refs[3 : 3 + len(pieces)]
        active_ref, hidden_grad_ref, terms_ref, field, filters = refs[3 + len(pieces) :]
        for ref, (_, parts) in zip(piece_refs, pieces):
            for first, slots, step, other in parts:
                base = owner_row(step, other, in_chan)
                for index, slot in enumerate(slots):
                    low = first + index * in_chan
                    field[pl.ds(slot * inputs + base, in_chan), :] = ref[low : low + in_chan, :]
        filters[...] = jnp.zeros_like(filters)
        places = []
        for tap, (depth_k, row_k, col_k) in enumerate(OFFSETS):
            top = roll_class(row_k, col_k) * outputs
            left = ((depth_k + 1) * 4 + phase_of(row_k, col_k)) * inputs
            places.append((slice(top, top + outputs), slice(left, left + inputs)))
            filters[places[-1]] = conv_ref[tap]
        terms = jnp.zeros((4 * outputs, depth), F32)
        actives = []
        for z in range(planes):
            view = field[8 * inputs * z : 8 * inputs * z + depth, :]
            sums = jnp.dot(filters[...], view, preferred_element_type=F32)
            hidden = sums[:outputs]
            for kind, (row_k, col_k) in ((1, (0, -1)), (2, (-1, 0)), (3, (-1, -1))):
                part = sums[kind * outputs : (kind + 1) * outputs]
                hidden = hidden + shift_cells(part, row_k, col_k, side)
            sigmoid = 1.0 / (1.0 + jnp.exp(-hidden))
            active = (hidden * sigmoid).astype(BF16)
            at = slice(z * square, (z + 1) * square)
            slope = sigmoid * (1.0 + hidden * (1.0 - sigmoid))
            grad = grad_ref[:, at] * slope
            active_ref[:, at] = active
            actives.append(active)
            rounded = grad.astype(BF16)
            hidden_grad_ref[z * outputs : (z + 1) * outputs, :] = rounded
            grad = rounded.astype(F32)
            shifted = jnp.concatenate(
                [shift_cells(grad, row_k, col_k, side) for row_k in (0, 1) for col_k in (0, 1)],
                axis=0,
            ).astype(BF16)
            terms = terms + lax.dot_general(
                shifted, view, (((1,), (1,)), ((), ())), preferred_element_type=F32
            )
        for tap, at in enumerate(places):
            terms_ref[tap * outputs : (tap + 1) * outputs, :] = terms[at].astype(BF16)
        pairs = lax.dot_general(
            jnp.concatenate(actives, axis=1),
            windows_ref[...],
            (((1,), (1,)), ((), ())),
            preferred_element_type=F32,
        )
        group = lax.broadcasted_iota(jnp.int32, (width, filter_rows), 1) % outputs // width
        kept = jnp.zeros((width, filter_rows), F32)
        for index in range(outputs // width):
            block = pairs[index * width : (index + 1) * width]
            kept = kept + jnp.where(group == index, block, 0.0)
        short = group_rows // width * 128 - filter_rows
        kept = jnp.concatenate([kept, jnp.zeros((width, short), F32)], axis=1)
        tail = [kept[:, 128 * i : 128 * (i + 1)] for i in range(group_rows // width)]
        tail.append(jnp.zeros((rows - filter_rows - group_rows, 128), F32))
        terms_ref[filter_rows:, :] = jnp.concatenate(tail, axis=0).astype(BF16)

    return call(
        kernel,
        (
            jax.ShapeDtypeStruct((outputs, cells), BF16),
            jax.ShapeDtypeStruct((planes * outputs, square), BF16),
            jax.ShapeDtypeStruct((rows, 128), BF16),
        ),
        conv_in,
        act_grad,
        windows,
        *[piece for piece, _ in pieces],
        scratch=[
            pltpu.VMEM((frames * 4 * inputs, square), BF16),
            pltpu.VMEM((4 * outputs, depth), BF16),
        ],
    )


def input_part(pieces, active, width, side):
    square = side * side
    outputs, cells = active.shape
    planes = cells // square
    devices = lax.axis_size("chan")

    def kernel(active_ref, *refs):
        piece_refs = refs[: len(pieces)]
        out_ref, down_ref, grads, filters = refs[len(pieces) :]
        for ref, (_, parts) in zip(piece_refs, pieces):
            for first, is_filter, step, other in parts:
                at = pl.ds(owner_row(step, other, outputs), outputs)
                target = filters if is_filter else grads
                for z in range(target.shape[1] // square):
                    low = first + z * outputs
                    target[at, z * square : (z + 1) * square] = ref[low : low + outputs, :]
        terms = lax.dot_general(
            filters[...], grads[...], (((0,), (0,)), ((), ())), preferred_element_type=F32
        )
        sums = {}
        for tap, (depth_k, row_k, col_k) in enumerate(OFFSETS):
            for z in range(planes):
                key = (2 * z + depth_k, phase_of(row_k, col_k), roll_class(row_k, col_k))
                part = terms[tap * width : (tap + 1) * width, z * square : (z + 1) * square]
                sums[key] = sums[key] + part if key in sums else part
        total = {}
        for (frame, phase, kind), part in sums.items():
            part = shift_cells(part, kind // 2, kind % 2, side)
            key = (frame, phase)
            total[key] = total[key] + part if key in total else part
        for (frame, phase), part in total.items():
            if frame < 0:
                down_ref[phase * width : (phase + 1) * width, :] = part.astype(BF16)
            else:
                out_ref[frame, :, phase * square : (phase + 1) * square] = part
        down_ref[4 * width :, :] = active_ref[:, :square]

    return call(
        kernel,
        (
            jax.ShapeDtypeStruct((2 * planes, width, 4 * square), F32),
            jax.ShapeDtypeStruct((4 * width + outputs, square), BF16),
        ),
        active,
        *[piece for piece, _ in pieces],
        scratch=[
            pltpu.VMEM((devices * outputs, cells), BF16),
            pltpu.VMEM((devices * outputs, 2 * square), BF16),
        ],
    )


def mix_part(low, active, packed, framed_grad, group_filter, side):
    outputs, cells = active.shape
    square = side * side
    planes = cells // square
    taps, width, _ = group_filter.shape
    in_planes, in_chan, _ = framed_grad.shape

    def kernel(low_ref, mid_ref, packed_ref, grad_ref, group_ref, out_ref, sum_ref, windows_ref):
        def store(tap, inner, window):
            windows_ref[
                tap * outputs : (tap + 1) * outputs, inner * square : (inner + 1) * square
            ] = window

        middle = [mid_ref[:, z * square : (z + 1) * square] for z in range(planes)]
        fill_windows([low_ref[...]] + middle + [packed_ref[4 * in_chan :, :]], store, 1, side)
        weights = jnp.concatenate(
            [block_diagonal(group_ref[tap].astype(F32), outputs) for tap in range(taps)], axis=0
        ).astype(BF16)
        mixed = lax.dot_general(
            weights, windows_ref[...], (((0,), (0,)), ((), ())), preferred_element_type=F32
        ).astype(BF16)
        for z in range(planes):
            out_ref[:, z, :] = mixed[:, z * square : (z + 1) * square]
        for frame in range(in_planes - 1):
            sum_ref[:, frame, :] = grad_ref[frame]
        for phase in range(4):
            at = slice(phase * square, (phase + 1) * square)
            from_above = packed_ref[phase * in_chan : (phase + 1) * in_chan, :].astype(F32)
            sum_ref[:, in_planes - 1, at] = grad_ref[in_planes - 1, :, at] + from_above

    return call(
        kernel,
        (
            jax.ShapeDtypeStruct((outputs, planes, square), BF16),
            jax.ShapeDtypeStruct((in_chan, in_planes, 4 * square), F32),
        ),
        low,
        active,
        packed,
        framed_grad,
        group_filter,
        scratch=[pltpu.VMEM((taps * outputs, cells), BF16)],
    )


def sum_part(received, scale):
    devices, rows, lanes = received.shape

    def kernel(src, dst):
        total = src[0].astype(F32)
        for index in range(1, devices):
            total = total + src[index].astype(F32)
        total = total * scale
        total = total.astype(BF16)
        for index in range(devices):
            dst[index] = total

    return call(kernel, jax.ShapeDtypeStruct(received.shape, BF16), received)


def final_part(gathered, taps, outputs, width):
    rows = taps * outputs
    blocks = -(-rows // 128)

    def kernel(src, filter_ref, group_ref):
        filter_ref[...] = src[:rows, :].astype(F32).reshape(taps, outputs, 128)
        tail = src[rows:, :].astype(F32)
        flat = jnp.concatenate(
            [tail[i * width : (i + 1) * width, :] for i in range(blocks)], axis=1
        )
        for tap in range(taps):
            group_ref[tap] = flat[:, tap * outputs : (tap + 1) * outputs]

    return call(
        kernel,
        (
            jax.ShapeDtypeStruct((taps, outputs, 128), F32),
            jax.ShapeDtypeStruct((taps, width, outputs), F32),
        ),
        gathered,
    )


def body(volume, conv_in, conv_group, cotangent):
    in_chan, in_planes, flat_in = volume.shape
    side = math.isqrt(flat_in) // 2
    square = side * side
    planes = in_planes // 2
    cells = planes * square
    taps, outputs, inputs = conv_in.shape
    width = conv_group.shape[2]
    slabs = lax.axis_size("space")
    blocks = lax.axis_size("chan")

    def along_space(block, step):
        return lax.ppermute(block, "space", [(i, (i + step) % slabs) for i in range(slabs)])

    def along_chips(block, step):
        return lax.ppermute(
            block, "chan", [(i, (i + 2 * step) % blocks) for i in range(blocks)]
        )

    def other_core(block):
        return lax.ppermute(block, "chan", [(i, i ^ 1) for i in range(blocks)])

    def joined(*parts):
        return jnp.concatenate(parts, axis=0)

    own, packed, upstream = prep_part(volume, cotangent)
    frame = 4 * in_chan
    packed = along_space(packed, 1)
    up_high = along_space(upstream[:outputs], -1)
    group_filter = jnp.transpose(conv_group, (0, 2, 1))
    act_grad, windows = upstream_part(packed, upstream, up_high, group_filter, side)
    sent = split_filter(conv_in, in_chan, square)

    slots = list(range(4 * (in_planes + 1)))
    length = len(slots) * in_chan
    cut = len(slots) // 2
    framed = joined(packed[:frame], own)
    from_low = along_chips(framed, 1)
    from_high = along_chips(framed, -1)
    from_low, sent = lax.optimization_barrier((from_low, sent))
    far_low = along_chips(from_low[: cut * in_chan], 1)
    far_high = along_chips(from_high[cut * in_chan :], -1)
    near_other = other_core(joined(from_low, from_high))
    low_other, high_other = other_core(far_low), other_core(far_high)
    pieces = [
        (framed, [(0, slots, 0, False)]),
        (other_core(framed), [(0, slots, 0, True)]),
        (from_low, [(0, slots, -1, False)]),
        (from_high, [(0, slots, 1, False)]),
        (near_other, [(0, slots, -1, True), (length, slots, 1, True)]),
        (far_low, [(0, slots[:cut], 2, False)]),
        (far_high, [(0, slots[cut:], 2, False)]),
        (low_other, [(0, slots[:cut], 2, True)]),
        (high_other, [(0, slots[cut:], 2, True)]),
    ]

    rows = -(-(taps * outputs + 64) // (slabs * 32)) * slabs * 32
    active, hidden_grad, terms = main_part(
        pieces, conv_in, act_grad, windows, width, rows, side
    )
    received = lax.all_to_all(
        terms.reshape(slabs, rows // slabs, 128), "space", split_axis=0, concat_axis=0, tiled=True
    )
    here, up, down, far = sent
    act_low = along_space(active[:, cells - square :], 1)
    up = along_chips(joined(hidden_grad, up), 1)
    down = along_chips(joined(hidden_grad, down), -1)
    far = along_chips(joined(hidden_grad, far), 2)
    block = 2 * outputs
    near = other_core(joined(hidden_grad, here[:block]))
    up, near = lax.optimization_barrier((up, near))
    crossed = other_core(
        joined(*[part for ring in (up, down, far) for part in (ring[:block], ring[2 * block :])])
    )
    steps = (-1, 1, 2)
    grads = [
        (hidden_grad, [(0, False, 0, False)]),
        (here, [(block, True, 0, False)]),
        (near, [(0, False, 0, True), (block, True, 0, True)]),
        (crossed, [(i * 2 * block, False, step, True) for i, step in enumerate(steps)]
         + [((2 * i + 1) * block, True, step, True) for i, step in enumerate(steps)]),
    ]
    for ring, step in zip((up, down, far), steps):
        grads.append((ring, [(0, False, step, False), (block, True, step, False)]))
    framed_grad, lowest = input_part(grads, active, in_chan, side)
    received, lowest, act_low = lax.optimization_barrier((received, lowest, act_low))
    scale = 1.0 / math.sqrt(slabs * cells)
    gathered = lax.all_to_all(
        sum_part(received, scale), "space", split_axis=0, concat_axis=0, tiled=True
    )
    filter_grad, group_grad = final_part(gathered.reshape(rows, 128), taps, outputs, width)

    mixed, input_grad = mix_part(
        act_low, active, along_space(lowest, -1), framed_grad, group_filter, side
    )
    return (
        mixed,
        input_grad,
        filter_grad,
        jnp.transpose(group_grad, (0, 2, 1)),
    )


def solution(mesh):
    return jax.shard_map(
        body,
        mesh=mesh,
        in_specs=(
            P("chan", "space", None),
            P(None, "chan", None),
            P(None, "chan", None),
            P("chan", "space", None),
        ),
        out_specs=(
            P("chan", "space", None),
            P("chan", "space", None),
            P(None, "chan", None),
            P(None, "chan", None),
        ),
        check_vma=False,
    )
```

```python
import math

import jax
import jax.numpy as jnp
from jax import lax
from jax.experimental import pallas as pl
from jax.experimental.pallas import tpu as pltpu
from jax.sharding import PartitionSpec as P

OFFSETS = [
    (first, second, third) for first in (-1, 0, 1) for second in (-1, 0, 1) for third in (-1, 0, 1)
]
TAPS = len(OFFSETS)
BF16 = jnp.bfloat16
F32 = jnp.float32
VMEM_LIMIT = 16 * 1024 * 1024


def phase_of(row_k, col_k):
    return 2 * (row_k != 0) + (col_k != 0)


def roll_class(row_k, col_k):
    return 2 * (row_k < 0) + (col_k < 0)


def shift_cells(plane, row_k, col_k, side):
    square = side * side
    moved = plane
    if col_k:
        inside = pltpu.roll(moved, (-col_k) % square, 1)
        wrapped = pltpu.roll(moved, (col_k * (side - 1)) % square, 1)
        column = lax.broadcasted_iota(jnp.int32, moved.shape, 1) % side
        moved = jnp.where(column == (side - 1 if col_k > 0 else 0), wrapped, inside)
    if row_k:
        moved = pltpu.roll(moved, (-row_k * side) % square, 1)
    return moved


def call(kernel, outs, *args, scratch=(), flops=0, moved=0):
    whole = pl.BlockSpec(memory_space=pltpu.VMEM)
    single = not isinstance(outs, (tuple, list))
    return pl.pallas_call(
        kernel,
        out_shape=outs,
        in_specs=[whole] * len(args),
        out_specs=whole if single else [whole] * len(outs),
        scratch_shapes=list(scratch),
        compiler_params=pltpu.CompilerParams(vmem_limit_bytes=VMEM_LIMIT),
        cost_estimate=pl.CostEstimate(flops=flops, bytes_accessed=moved, transcendentals=0),
    )(*args)


def prep_part(volume, cotangent):
    in_chan, in_planes, flat_in = volume.shape
    outputs, planes, square = cotangent.shape

    def kernel(vol_ref, cot_ref, own_ref, packed_ref, cells_ref):
        for frame in range(in_planes):
            for phase in range(4):
                low = (frame * 4 + phase) * in_chan
                part = vol_ref[frame, :, phase * square : (phase + 1) * square]
                own_ref[low : low + in_chan, :] = part
                if frame == in_planes - 1:
                    packed_ref[phase * in_chan : (phase + 1) * in_chan, :] = part
        for z in range(planes):
            cells_ref[z * outputs : (z + 1) * outputs, :] = cot_ref[z]
        packed_ref[4 * in_chan :, :] = cot_ref[planes - 1]

    return call(
        kernel,
        (
            jax.ShapeDtypeStruct((in_planes * 4 * in_chan, square), BF16),
            jax.ShapeDtypeStruct((4 * in_chan + outputs, square), BF16),
            jax.ShapeDtypeStruct((planes * outputs, square), BF16),
        ),
        jnp.transpose(volume, (1, 0, 2)),
        jnp.transpose(cotangent, (1, 0, 2)),
    )


def split_filter(conv_in, in_chan, square):
    taps, outputs, inputs = conv_in.shape
    count = inputs // in_chan
    block_rows = 2 * outputs
    short = 2 * square - taps * in_chan

    def kernel(conv_ref, here_ref, up_ref, down_ref, far_ref, blocks):
        me = lax.axis_index("chan")
        for owner in range(count):
            steps = lax.rem(owner // 2 + count // 2 - me // 2, count // 2)
            crossed = lax.rem(owner + me, 2)
            wide = [conv_ref[tap, :, owner * in_chan : (owner + 1) * in_chan] for tap in range(taps)]
            wide = jnp.concatenate(wide + [jnp.zeros((outputs, short), BF16)], axis=1)
            blocks[2 * steps + crossed, :outputs, :] = wide[:, :square]
            blocks[2 * steps + crossed, outputs:, :] = wide[:, square:]
        for ref, order in ((here_ref, (1, 0)), (up_ref, (2, 3)), (down_ref, (6, 7)), (far_ref, (4, 5))):
            for index, block in enumerate(order):
                ref[index * block_rows : (index + 1) * block_rows, :] = blocks[block]

    return call(
        kernel,
        [jax.ShapeDtypeStruct((2 * block_rows, square), BF16)] * 4,
        conv_in,
        scratch=[pltpu.VMEM((count, block_rows, square), BF16)],
    )


def fill_windows(planes, store, direction, side):
    count = len(planes) - 2
    for index, plane in enumerate(planes):
        plane = plane.astype(F32)
        for row_k in (-1, 0, 1):
            for col_k in (-1, 0, 1):
                window = shift_cells(plane, direction * row_k, direction * col_k, side).astype(BF16)
                for depth_k in (-1, 0, 1):
                    inner = index - 1 - direction * depth_k
                    if 0 <= inner < count:
                        tap = 9 * (depth_k + 1) + 3 * (row_k + 1) + col_k + 1
                        store(tap, inner, window)


def block_diagonal(values, outputs):
    width, columns = values.shape
    tiled = jnp.concatenate([values] * (outputs // width), axis=0)
    row = lax.broadcasted_iota(jnp.int32, tiled.shape, 0)
    column = lax.broadcasted_iota(jnp.int32, tiled.shape, 1) % outputs
    return jnp.where(row // width == column // width, tiled, jnp.zeros_like(tiled))


def upstream_part(packed, cotangent, high, group_filter, side):
    square = side * side
    taps, width, outputs = group_filter.shape
    planes = cotangent.shape[0] // outputs
    cells = planes * square
    skipped = packed.shape[0] - outputs

    def kernel(low_ref, mid_ref, high_ref, group_ref, grad_ref, windows_ref):
        def store(tap, inner, window):
            windows_ref[
                tap * outputs : (tap + 1) * outputs, inner * square : (inner + 1) * square
            ] = window

        middle = [mid_ref[z * outputs : (z + 1) * outputs, :] for z in range(planes)]
        fill_windows([low_ref[skipped:, :]] + middle + [high_ref[...]], store, -1, side)
        flat = jnp.concatenate([group_ref[tap].astype(F32) for tap in range(taps)], axis=1)
        weights = block_diagonal(flat, outputs).astype(BF16)
        grad_ref[...] = jnp.dot(weights, windows_ref[...], preferred_element_type=F32)

    return call(
        kernel,
        (
            jax.ShapeDtypeStruct((outputs, cells), F32),
            jax.ShapeDtypeStruct((taps * outputs, cells), BF16),
        ),
        packed,
        cotangent,
        high,
        group_filter,
        flops=10**10,
    )


def owner_row(step, other, rows):
    me = lax.axis_index("chan")
    count = lax.axis_size("chan")
    owner = lax.rem(me + (2 * step) % count, count)
    if other:
        owner = owner + 1 - 2 * lax.rem(owner, 2)
    return pl.multiple_of(owner * rows, rows)


def main_part(pieces, conv_in, act_grad, windows, width, rows, side):
    taps, outputs, inputs = conv_in.shape
    square = side * side
    cells = act_grad.shape[1]
    planes = cells // square
    frames = 2 * planes + 1
    depth = 12 * inputs
    in_chan = inputs // lax.axis_size("chan")
    filter_rows = taps * outputs
    group_rows = -(-filter_rows // 128) * width

    def kernel(*refs):
        conv_ref, grad_ref, windows_ref = refs[:3]
        piece_refs = refs[3 : 3 + len(pieces)]
        active_ref, hidden_grad_ref, terms_ref, field, filters = refs[3 + len(pieces) :]
        for ref, (_, parts) in zip(piece_refs, pieces):
            for first, slots, step, other in parts:
                base = owner_row(step, other, in_chan)
                for index, slot in enumerate(slots):
                    low = first + index * in_chan
                    field[pl.ds(slot * inputs + base, in_chan), :] = ref[low : low + in_chan, :]
        filters[...] = jnp.zeros_like(filters)
        places = []
        for tap, (depth_k, row_k, col_k) in enumerate(OFFSETS):
            top = roll_class(row_k, col_k) * outputs
            left = ((depth_k + 1) * 4 + phase_of(row_k, col_k)) * inputs
            places.append((slice(top, top + outputs), slice(left, left + inputs)))
            filters[places[-1]] = conv_ref[tap]
        terms = jnp.zeros((4 * outputs, depth), F32)
        actives = []
        for z in range(planes):
            view = field[8 * inputs * z : 8 * inputs * z + depth, :]
            sums = jnp.dot(filters[...], view, preferred_element_type=F32)
            hidden = sums[:outputs]
            for kind, (row_k, col_k) in ((1, (0, -1)), (2, (-1, 0)), (3, (-1, -1))):
                part = sums[kind * outputs : (kind + 1) * outputs]
                hidden = hidden + shift_cells(part, row_k, col_k, side)
            sigmoid = 1.0 / (1.0 + jnp.exp(-hidden))
            active = (hidden * sigmoid).astype(BF16)
            at = slice(z * square, (z + 1) * square)
            slope = sigmoid * (1.0 + hidden * (1.0 - sigmoid))
            grad = grad_ref[:, at] * slope
            active_ref[:, at] = active
            actives.append(active)
            rounded = grad.astype(BF16)
            hidden_grad_ref[z * outputs : (z + 1) * outputs, :] = rounded
            grad = rounded.astype(F32)
            shifted = jnp.concatenate(
                [shift_cells(grad, row_k, col_k, side) for row_k in (0, 1) for col_k in (0, 1)],
                axis=0,
            ).astype(BF16)
            terms = terms + lax.dot_general(
                shifted, view, (((1,), (1,)), ((), ())), preferred_element_type=F32
            )
        for tap, at in enumerate(places):
            terms_ref[tap * outputs : (tap + 1) * outputs, :] = terms[at].astype(BF16)
        pairs = lax.dot_general(
            jnp.concatenate(actives, axis=1),
            windows_ref[...],
            (((1,), (1,)), ((), ())),
            preferred_element_type=F32,
        )
        group = lax.broadcasted_iota(jnp.int32, (width, filter_rows), 1) % outputs // width
        kept = jnp.zeros((width, filter_rows), F32)
        for index in range(outputs // width):
            block = pairs[index * width : (index + 1) * width]
            kept = kept + jnp.where(group == index, block, 0.0)
        short = group_rows // width * 128 - filter_rows
        kept = jnp.concatenate([kept, jnp.zeros((width, short), F32)], axis=1)
        tail = [kept[:, 128 * i : 128 * (i + 1)] for i in range(group_rows // width)]
        tail.append(jnp.zeros((rows - filter_rows - group_rows, 128), F32))
        terms_ref[filter_rows:, :] = jnp.concatenate(tail, axis=0).astype(BF16)

    return call(
        kernel,
        (
            jax.ShapeDtypeStruct((outputs, cells), BF16),
            jax.ShapeDtypeStruct((planes * outputs, square), BF16),
            jax.ShapeDtypeStruct((rows, 128), BF16),
        ),
        conv_in,
        act_grad,
        windows,
        *[piece for piece, _ in pieces],
        scratch=[
            pltpu.VMEM((frames * 4 * inputs, square), BF16),
            pltpu.VMEM((4 * outputs, depth), BF16),
        ],
    )


def input_part(pieces, active, width, side):
    square = side * side
    outputs, cells = active.shape
    planes = cells // square
    devices = lax.axis_size("chan")

    def kernel(active_ref, *refs):
        piece_refs = refs[: len(pieces)]
        out_ref, down_ref, grads, filters = refs[len(pieces) :]
        for ref, (_, parts) in zip(piece_refs, pieces):
            for first, is_filter, step, other in parts:
                at = pl.ds(owner_row(step, other, outputs), outputs)
                target = filters if is_filter else grads
                for z in range(target.shape[1] // square):
                    low = first + z * outputs
                    target[at, z * square : (z + 1) * square] = ref[low : low + outputs, :]
        terms = lax.dot_general(
            filters[...], grads[...], (((0,), (0,)), ((), ())), preferred_element_type=F32
        )
        sums = {}
        for tap, (depth_k, row_k, col_k) in enumerate(OFFSETS):
            for z in range(planes):
                key = (2 * z + depth_k, phase_of(row_k, col_k), roll_class(row_k, col_k))
                part = terms[tap * width : (tap + 1) * width, z * square : (z + 1) * square]
                sums[key] = sums[key] + part if key in sums else part
        total = {}
        for (frame, phase, kind), part in sums.items():
            part = shift_cells(part, kind // 2, kind % 2, side)
            key = (frame, phase)
            total[key] = total[key] + part if key in total else part
        for (frame, phase), part in total.items():
            if frame < 0:
                down_ref[phase * width : (phase + 1) * width, :] = part.astype(BF16)
            else:
                out_ref[frame, :, phase * square : (phase + 1) * square] = part
        down_ref[4 * width :, :] = active_ref[:, :square]

    return call(
        kernel,
        (
            jax.ShapeDtypeStruct((2 * planes, width, 4 * square), F32),
            jax.ShapeDtypeStruct((4 * width + outputs, square), BF16),
        ),
        active,
        *[piece for piece, _ in pieces],
        scratch=[
            pltpu.VMEM((devices * outputs, cells), BF16),
            pltpu.VMEM((devices * outputs, 2 * square), BF16),
        ],
    )


def mix_part(low, active, packed, framed_grad, group_filter, side):
    outputs, cells = active.shape
    square = side * side
    planes = cells // square
    taps, width, _ = group_filter.shape
    in_planes, in_chan, _ = framed_grad.shape

    def kernel(low_ref, mid_ref, packed_ref, grad_ref, group_ref, out_ref, sum_ref, windows_ref):
        def store(tap, inner, window):
            windows_ref[
                tap * outputs : (tap + 1) * outputs, inner * square : (inner + 1) * square
            ] = window

        middle = [mid_ref[:, z * square : (z + 1) * square] for z in range(planes)]
        fill_windows([low_ref[...]] + middle + [packed_ref[4 * in_chan :, :]], store, 1, side)
        weights = jnp.concatenate(
            [block_diagonal(group_ref[tap].astype(F32), outputs) for tap in range(taps)], axis=0
        ).astype(BF16)
        mixed = lax.dot_general(
            weights, windows_ref[...], (((0,), (0,)), ((), ())), preferred_element_type=F32
        ).astype(BF16)
        for z in range(planes):
            out_ref[:, z, :] = mixed[:, z * square : (z + 1) * square]
        for frame in range(in_planes - 1):
            sum_ref[:, frame, :] = grad_ref[frame]
        for phase in range(4):
            at = slice(phase * square, (phase + 1) * square)
            from_above = packed_ref[phase * in_chan : (phase + 1) * in_chan, :].astype(F32)
            sum_ref[:, in_planes - 1, at] = grad_ref[in_planes - 1, :, at] + from_above

    return call(
        kernel,
        (
            jax.ShapeDtypeStruct((outputs, planes, square), BF16),
            jax.ShapeDtypeStruct((in_chan, in_planes, 4 * square), F32),
        ),
        low,
        active,
        packed,
        framed_grad,
        group_filter,
        scratch=[pltpu.VMEM((taps * outputs, cells), BF16)],
    )


def sum_part(received, scale):
    devices, rows, lanes = received.shape

    def kernel(src, dst):
        total = src[0].astype(F32)
        for index in range(1, devices):
            total = total + src[index].astype(F32)
        total = total * scale
        total = total.astype(BF16)
        for index in range(devices):
            dst[index] = total

    return call(kernel, jax.ShapeDtypeStruct(received.shape, BF16), received)


def final_part(gathered, taps, outputs, width):
    rows = taps * outputs
    blocks = -(-rows // 128)

    def kernel(src, filter_ref, group_ref):
        filter_ref[...] = src[:rows, :].astype(F32).reshape(taps, outputs, 128)
        tail = src[rows:, :].astype(F32)
        flat = jnp.concatenate(
            [tail[i * width : (i + 1) * width, :] for i in range(blocks)], axis=1
        )
        for tap in range(taps):
            group_ref[tap] = flat[:, tap * outputs : (tap + 1) * outputs]

    return call(
        kernel,
        (
            jax.ShapeDtypeStruct((taps, outputs, 128), F32),
            jax.ShapeDtypeStruct((taps, width, outputs), F32),
        ),
        gathered,
    )


def body(volume, conv_in, conv_group, cotangent):
    in_chan, in_planes, flat_in = volume.shape
    side = math.isqrt(flat_in) // 2
    square = side * side
    planes = in_planes // 2
    cells = planes * square
    taps, outputs, inputs = conv_in.shape
    width = conv_group.shape[2]
    slabs = lax.axis_size("space")
    blocks = lax.axis_size("chan")

    def along_space(block, step):
        return lax.ppermute(block, "space", [(i, (i + step) % slabs) for i in range(slabs)])

    def along_chips(block, step):
        return lax.ppermute(
            block, "chan", [(i, (i + 2 * step) % blocks) for i in range(blocks)]
        )

    def other_core(block):
        return lax.ppermute(block, "chan", [(i, i ^ 1) for i in range(blocks)])

    def joined(*parts):
        return jnp.concatenate(parts, axis=0)

    own, packed, upstream = prep_part(volume, cotangent)
    frame = 4 * in_chan
    packed = along_space(packed, 1)
    up_high = along_space(upstream[:outputs], -1)
    group_filter = jnp.transpose(conv_group, (0, 2, 1))
    act_grad, windows = upstream_part(packed, upstream, up_high, group_filter, side)
    sent = split_filter(conv_in, in_chan, square)

    slots = list(range(4 * (in_planes + 1)))
    length = len(slots) * in_chan
    cut = len(slots) // 2
    framed = joined(packed[:frame], own)
    from_low = along_chips(framed, 1)
    from_high = along_chips(framed, -1)
    from_low, sent = lax.optimization_barrier((from_low, sent))
    far_low = along_chips(from_low[: cut * in_chan], 1)
    far_high = along_chips(from_high[cut * in_chan :], -1)
    near_other = other_core(joined(from_low, from_high))
    far_other = other_core(joined(far_low, far_high))
    pieces = [
        (framed, [(0, slots, 0, False)]),
        (other_core(framed), [(0, slots, 0, True)]),
        (from_low, [(0, slots, -1, False)]),
        (from_high, [(0, slots, 1, False)]),
        (near_other, [(0, slots, -1, True), (length, slots, 1, True)]),
        (far_low, [(0, slots[:cut], 2, False)]),
        (far_high, [(0, slots[cut:], 2, False)]),
        (far_other, [(0, slots, 2, True)]),
    ]

    rows = -(-(taps * outputs + 64) // (slabs * 32)) * slabs * 32
    active, hidden_grad, terms = main_part(
        pieces, conv_in, act_grad, windows, width, rows, side
    )
    received = lax.all_to_all(
        terms.reshape(slabs, rows // slabs, 128), "space", split_axis=0, concat_axis=0, tiled=True
    )
    here, up, down, far = sent
    act_low = along_space(active[:, cells - square :], 1)
    up = along_chips(joined(hidden_grad, up), 1)
    down = along_chips(joined(hidden_grad, down), -1)
    far = along_chips(joined(hidden_grad, far), 2)
    block = 2 * outputs
    up, lent = lax.optimization_barrier((up, joined(hidden_grad, here[:block])))
    near = other_core(lent)
    crossed = other_core(
        joined(*[part for ring in (up, down, far) for part in (ring[:block], ring[2 * block :])])
    )
    steps = (-1, 1, 2)
    grads = [
        (hidden_grad, [(0, False, 0, False)]),
        (here, [(block, True, 0, False)]),
        (near, [(0, False, 0, True), (block, True, 0, True)]),
        (crossed, [(i * 2 * block, False, step, True) for i, step in enumerate(steps)]
         + [((2 * i + 1) * block, True, step, True) for i, step in enumerate(steps)]),
    ]
    for ring, step in zip((up, down, far), steps):
        grads.append((ring, [(0, False, step, False), (block, True, step, False)]))
    framed_grad, lowest = input_part(grads, active, in_chan, side)
    received, lowest, act_low = lax.optimization_barrier((received, lowest, act_low))
    scale = 1.0 / math.sqrt(slabs * cells)
    gathered = lax.all_to_all(
        sum_part(received, scale), "space", split_axis=0, concat_axis=0, tiled=True
    )
    filter_grad, group_grad = final_part(gathered.reshape(rows, 128), taps, outputs, width)

    mixed, input_grad = mix_part(
        act_low, active, along_space(lowest, -1), framed_grad, group_filter, side
    )
    return (
        mixed,
        input_grad,
        filter_grad,
        jnp.transpose(group_grad, (0, 2, 1)),
    )


def solution(mesh):
    return jax.shard_map(
        body,
        mesh=mesh,
        in_specs=(
            P("chan", "space", None),
            P(None, "chan", None),
            P(None, "chan", None),
            P("chan", "space", None),
        ),
        out_specs=(
            P("chan", "space", None),
            P("chan", "space", None),
            P(None, "chan", None),
            P(None, "chan", None),
        ),
        check_vma=False,
    )
```
